256 devices in a mesh: row: 2 (over x_hi), circ: 64 (over y, z, x_lo), rad: 2 (over core).
Axes of the slice: x: 4 (x_hi: 2, x_lo: 2; x = x_hi * 2 + x_lo), y: 4, z: 8, core: 2. Of those that a mesh axis runs over, the one named last changes fastest.
Arguments:
- state: float32 [2, 5, 8, 64, 8192], P('row', None, None, 'rad', 'circ'), as said below
- inv_volume: float32 [2, 8, 64, 8192], P('row', None, 'rad', 'circ'), may hold values from 0.5 to 2
- wheel_speed: float32 [64], P('rad'), may hold values from 0.2 to 0.6
- offset: int32 [1], replicated, may hold values from 0 to 8191
Outputs:
- new_state: float32 [2, 5, 8, 64, 8192], P('row', None, None, 'rad', 'circ')
- rate: float32 [2, 5, 8, 64, 8192], P('row', None, None, 'rad', 'circ')
The draws below stay inside these ranges and needn't reach their ends.
Inputs may be any that keep to these rules, and one draw needn't show every extreme that they name: `state`: density and pressure lie between 0.7 and 1.4, each velocity component within 0.9 in magnitude.
All inputs are finite; a program needn't handle non-finite values.
Results may differ from the reference program's by a relative error of at most 0.00002.
Values sent between devices are 32-bit elements; how exact they have to be, the bound alone decides.
A program may use at most 64 MiB of HBM per device.

```python
import math
import jax
import jax.numpy as jnp

AX_CELLS = 8
NR = 64
NC = 8192


GAMMA = 1.4


def draw_state(key, part):
    key = jax.random.fold_in(key, 11)
    keys = jax.random.split(key, 5)
    shape = (2, AX_CELLS, NR, NC)
    density = jnp.exp(jax.random.uniform(keys[0], shape, jnp.float32, math.log(0.7), math.log(1.4)))
    pressure = jnp.exp(jax.random.uniform(keys[1], shape, jnp.float32, math.log(0.7), math.log(1.4)))
    axial = jnp.clip(0.3 * jax.random.normal(keys[2], shape, jnp.float32), -0.9, 0.9)
    radial = jnp.clip(0.3 * jax.random.normal(keys[3], shape, jnp.float32), -0.9, 0.9)
    circum = jnp.clip(0.3 * jax.random.normal(keys[4], shape, jnp.float32), -0.9, 0.9)
    energy = pressure / (GAMMA - 1.0) + 0.5 * density * (axial * axial + radial * radial + circum * circum)
    return jnp.stack([density, density * axial, density * radial, density * circum, energy], axis=1)


def level_of(rng, dims, pieces, least, largest):
    factor_of = 1.0
    for position, blocks in pieces:
        steps = jax.random.uniform(jax.random.fold_in(jax.random.fold_in(rng, 6), position), (blocks,), jnp.float32, least / len(pieces), largest / len(pieces))
        factor_of = factor_of * jnp.repeat(jnp.exp(steps), dims[position] // blocks).reshape((-1,) + (1,) * (len(dims) - 1 - position))
    return factor_of


def setup_inputs(seed: int = 0) -> dict:
    streams_of = jax.random.split(jax.random.key(seed), 5)
    return {
        "state": draw_state(jax.random.fold_in(streams_of[4], 71), 0),
        "inv_volume": jnp.clip(jnp.exp(math.log(2.0) - 1.3862944 * jax.random.uniform(streams_of[1], (2, AX_CELLS, NR, NC), jnp.float32) ** level_of(streams_of[1], (2, AX_CELLS, NR, NC), ((0, 2), (2, 2), (3, 64)), -0.2, 0.2)), 0.5, 2.0),
        "wheel_speed": jnp.clip(0.2 + 0.400000021 * jax.random.uniform(streams_of[2], (NR,), jnp.float32) ** level_of(streams_of[2], (NR,), ((0, 2),), -0.2, 0.2), 0.2, 0.6),
        "offset": jax.random.randint(streams_of[3], (1,), 0, NC).astype(jnp.int32),
    }


GAMMA = 1.4
TIME_STEP = 0.05

def euler_flux(cells, component):
    density = cells[0]
    normal_speed = cells[component] / density
    kinetic = 0.5 * (cells[1] * cells[1] + cells[2] * cells[2] + cells[3] * cells[3]) / density
    pressure = (GAMMA - 1.0) * (cells[4] - kinetic)
    flux = cells * normal_speed[None]
    flux = flux.at[component].add(pressure)
    flux = flux.at[4].add(pressure * normal_speed)
    wave = jnp.abs(normal_speed) + jnp.sqrt(GAMMA * pressure / density)
    return (flux, wave)

def face_flux(left, right, component):
    flux_left, wave_left = euler_flux(left, component)
    flux_right, wave_right = euler_flux(right, component)
    return 0.5 * (flux_left + flux_right) - 0.5 * jnp.maximum(wave_left, wave_right)[None] * (right - left)

def divergence(padded_axial, padded_radial, padded_circ, inv_volume):
    axial = face_flux(padded_axial[:, :-1], padded_axial[:, 1:], 1)
    radial = face_flux(padded_radial[:, :, :-1], padded_radial[:, :, 1:], 2)
    circum = face_flux(padded_circ[..., :-1], padded_circ[..., 1:], 3)
    total = axial[:, 1:] - axial[:, :-1] + (radial[:, :, 1:] - radial[:, :, :-1]) + (circum[..., 1:] - circum[..., :-1])
    return -inv_volume[None] * total

def to_absolute(layer, wheel):
    density = layer[0]
    moment = layer[3]
    return jnp.stack([layer[0], layer[1], layer[2], moment + density * wheel, layer[4] + moment * wheel + 0.5 * density * wheel * wheel])

def to_relative(layer, wheel):
    density = layer[0]
    moment = layer[3]
    return jnp.stack([layer[0], layer[1], layer[2], moment - density * wheel, layer[4] - moment * wheel + 0.5 * density * wheel * wheel])

def mirror(layer):
    signs = jnp.array([1.0, 1.0, -1.0, 1.0, 1.0], jnp.float32)[:, None, None, None]
    return layer * signs

def row_rate(cells, padded_axial, inv_volume):
    padded_radial = jnp.concatenate([mirror(cells[:, :, :1]), cells, mirror(cells[:, :, -1:])], 2)
    padded_circ = jnp.concatenate([cells[..., -1:], cells, cells[..., :1]], 3)
    return divergence(padded_axial, padded_radial, padded_circ, inv_volume)

def full_rate(state, inv_volume, wheel, shift):
    rotor = state[0]
    stator = state[1]
    positions = jnp.arange(NC, dtype=jnp.int32)
    rotor_ghost = to_relative(stator[:, 0], wheel)[..., (positions + shift) % NC]
    stator_ghost = to_absolute(rotor[:, -1], wheel)[..., (positions - shift + NC) % NC]
    rotor_axial = jnp.concatenate([rotor[:, :1], rotor, rotor_ghost[:, None]], 1)
    stator_axial = jnp.concatenate([stator_ghost[:, None], stator, stator[:, -1:]], 1)
    return jnp.stack([row_rate(rotor, rotor_axial, inv_volume[0]), row_rate(stator, stator_axial, inv_volume[1])])

def reference(state, inv_volume, wheel_speed, offset):
    wheel = wheel_speed[:, None]
    shift = offset[0]
    rate_zero = full_rate(state, inv_volume, wheel, shift)
    first = state + TIME_STEP * rate_zero
    rate = full_rate(first, inv_volume, wheel, shift)
    new_state = 0.5 * state + 0.5 * (first + TIME_STEP * rate)
    return (new_state, rate)
```

```python
import functools

import jax
import jax.numpy as jnp
from jax import lax
from jax.experimental import pallas as pl
from jax.experimental.pallas import tpu as pltpu
from jax.sharding import PartitionSpec as P

MESH = pl.DeviceIdType.MESH

GAMMA = 1.4
TIME_STEP = 0.05


def from_partner(array, axis, distance):
    return lax.ppermute(array, axis, [(i, i ^ 1 << distance) for i in range(lax.axis_size(axis))])


def passed_along(value, axis, steps):
    count = lax.axis_size(axis)
    pairs = [(source, (source + steps) % count) for source in range(count)]
    return lax.ppermute(value, axis, pairs)


def with_halo(array, sides, width, wrap):
    for axis, dim in sides:
        size, length = (lax.axis_size(axis), array.shape[dim])
        up = [(i, (i + 1) % size) for i in range(size if wrap else size - 1)]
        down = [(j, i) for i, j in up]
        last = lax.slice_in_dim(array, length - width, length, axis=dim)
        first = lax.slice_in_dim(array, 0, width, axis=dim)
        before = lax.ppermute(last, axis, up)
        after = lax.ppermute(first, axis, down)
        array = jnp.concatenate([before, array, after], axis=dim)
    return array


def euler_flux(cells, component):
    density = cells[0]
    normal_speed = cells[component] / density
    kinetic = 0.5 * (cells[1] * cells[1] + cells[2] * cells[2] + cells[3] * cells[3]) / density
    pressure = (GAMMA - 1.0) * (cells[4] - kinetic)
    flux = cells * normal_speed[None]
    flux = flux.at[component].add(pressure)
    flux = flux.at[4].add(pressure * normal_speed)
    wave = jnp.abs(normal_speed) + jnp.sqrt(GAMMA * pressure / density)
    return (flux, wave)


def face_flux(left, right, component):
    flux_left, wave_left = euler_flux(left, component)
    flux_right, wave_right = euler_flux(right, component)
    return 0.5 * (flux_left + flux_right) - 0.5 * jnp.maximum(wave_left, wave_right)[None] * (
        right - left
    )


def divergence(padded_axial, padded_radial, padded_circ, inv_volume):
    axial = face_flux(padded_axial[:, :-1], padded_axial[:, 1:], 1)
    radial = face_flux(padded_radial[:, :, :-1], padded_radial[:, :, 1:], 2)
    circum = face_flux(padded_circ[..., :-1], padded_circ[..., 1:], 3)
    total = (
        axial[:, 1:]
        - axial[:, :-1]
        + (radial[:, :, 1:] - radial[:, :, :-1])
        + (circum[..., 1:] - circum[..., :-1])
    )
    return -inv_volume[None] * total


def to_absolute(layer, wheel):
    density = layer[0]
    moment = layer[3]
    return jnp.stack(
        [
            layer[0],
            layer[1],
            layer[2],
            moment + density * wheel,
            layer[4] + moment * wheel + 0.5 * density * wheel * wheel,
        ]
    )


def to_relative(layer, wheel):
    density = layer[0]
    moment = layer[3]
    return jnp.stack(
        [
            layer[0],
            layer[1],
            layer[2],
            moment - density * wheel,
            layer[4] - moment * wheel + 0.5 * density * wheel * wheel,
        ]
    )


def mirror(layer):
    signs = jnp.array([1.0, 1.0, -1.0, 1.0, 1.0], jnp.float32)[:, None, None, None]
    return layer * signs


def exchange_kernel(shift, sectors, piece_ref, got_ref, send_sem, recv_sem):
    row = lax.axis_index("row")
    sector = lax.axis_index("circ")
    near = lax.rem(sector + jnp.where(row == 0, shift, sectors - shift), sectors)
    far = lax.rem(near + jnp.where(row == 0, 1, sectors - 1), sectors)
    targets = [{"row": 1 - row, "circ": near}, {"row": 1 - row, "circ": far}]
    barrier = pltpu.get_barrier_semaphore()
    for target in targets:
        pl.semaphore_signal(barrier, inc=1, device_id=target, device_id_type=MESH)
    pl.semaphore_wait(barrier, 2)
    copies = [
        pltpu.make_async_remote_copy(
            src_ref=piece_ref,
            dst_ref=got_ref.at[i],
            send_sem=send_sem.at[i],
            recv_sem=recv_sem.at[i],
            device_id=targets[i],
            device_id_type=MESH,
        )
        for i in range(2)
    ]
    for copy in copies:
        copy.start()
    for copy in copies:
        copy.wait()


def exchange(shift, call, piece):
    sectors = lax.axis_size("circ")
    return pl.pallas_call(
        functools.partial(exchange_kernel, shift, sectors),
        out_shape=jax.ShapeDtypeStruct((2,) + piece.shape, piece.dtype),
        in_specs=[pl.BlockSpec(memory_space=pltpu.VMEM)],
        out_specs=pl.BlockSpec(memory_space=pltpu.VMEM),
        scratch_shapes=[pltpu.SemaphoreType.DMA((2,)), pltpu.SemaphoreType.DMA((2,))],
        compiler_params=pltpu.CompilerParams(
            collective_id=call * sectors + shift, has_side_effects=True
        ),
    )(piece)


def plane_layer(cells, wheel, offset, call):
    row_index = lax.axis_index("row")
    sector_cells = cells.shape[3]
    sectors = lax.axis_size("circ")
    outgoing = jnp.where(
        row_index == 0, to_absolute(cells[:, -1], wheel), to_relative(cells[:, 0], wheel)
    )
    got = lax.switch(
        offset // sector_cells,
        [functools.partial(exchange, shift, call) for shift in range(sectors)],
        outgoing,
    )
    rest = offset % sector_cells
    low = jnp.where(row_index == 0, got[0], got[1])
    high = jnp.where(row_index == 0, got[1], got[0])
    start = jnp.where(row_index == 0, rest, sector_cells - rest)
    joined = jnp.concatenate([low, high], 2)
    return lax.dynamic_slice_in_dim(joined, start, sector_cells, 2)


def local_rate(cells, inv_volume, wheel, offset, call):
    row_index = lax.axis_index("row")
    rad_index = lax.axis_index("rad")
    ghost = plane_layer(cells, wheel, offset, call)[:, None]
    padded_axial = jnp.where(
        row_index == 0,
        jnp.concatenate([cells[:, :1], cells, ghost], 1),
        jnp.concatenate([ghost, cells, cells[:, -1:]], 1),
    )
    padded_circ = with_halo(cells, (("circ", 3),), 1, True)
    rimmed = with_halo(cells, (("rad", 2),), 1, False)
    lower = jnp.where(rad_index == 0, mirror(cells[:, :, :1]), rimmed[:, :, :1])
    upper = jnp.where(
        rad_index == lax.axis_size("rad") - 1, mirror(cells[:, :, -1:]), rimmed[:, :, -1:]
    )
    padded_radial = jnp.concatenate([lower, rimmed[:, :, 1:-1], upper], 2)
    return divergence(padded_axial, padded_radial, padded_circ, inv_volume)


def on_device(state, inv_volume, wheel_speed, offset):
    cells = state[0]
    volumes = inv_volume[0]
    wheel = wheel_speed[:, None]
    rate_zero = local_rate(cells, volumes, wheel, offset[0], 0)
    first = cells + TIME_STEP * rate_zero
    rate = local_rate(first, volumes, wheel, offset[0], 1)
    new_state = 0.5 * cells + 0.5 * (first + TIME_STEP * rate)
    return (new_state[None], rate[None])


def solution(mesh):
    return jax.shard_map(
        on_device,
        mesh=mesh,
        in_specs=(
            P("row", None, None, "rad", "circ"),
            P("row", None, "rad", "circ"),
            P("rad"),
            P(),
        ),
        out_specs=(P("row", None, None, "rad", "circ"), P("row", None, None, "rad", "circ")),
        check_vma=False,
    )
```

```python
import functools

import jax
import jax.numpy as jnp
from jax import lax
from jax.experimental import pallas as pl
from jax.experimental.pallas import tpu as pltpu
from jax.sharding import PartitionSpec as P

GAMMA = 1.4
TIME_STEP = 0.05
MESH = pl.DeviceIdType.MESH

V1, V2, V3, PRESSURE, SOUND = 5, 6, 7, 8, 9
QUANTITIES = 10
AXIAL = (0, 1, 2, 3, 4, V1, PRESSURE, SOUND)
RADIAL = (0, 1, 2, 3, 4, V2, PRESSURE, SOUND)
CIRCUM = (0, 1, 2, 3, 4, V3, PRESSURE, SOUND)
PAD = 8
PARTS = 1


def quantities(u):
    inverse = 1.0 / u[0]
    v1, v2, v3 = u[1] * inverse, u[2] * inverse, u[3] * inverse
    pressure = (GAMMA - 1.0) * (u[4] - 0.5 * (u[1] * v1 + u[2] * v2 + u[3] * v3))
    return list(u) + [v1, v2, v3, pressure, jnp.sqrt(GAMMA * pressure * inverse)]


def flux(cell, component):
    speed, pressure = cell[5], cell[6]
    out = [cell[c] * speed for c in range(4)] + [(cell[4] + pressure) * speed]
    out[component] = out[component] + pressure
    return out


def add_side(total, here, there, component, sign):
    wave = jnp.maximum(jnp.abs(here[5]) + here[7], jnp.abs(there[5]) + there[7])
    moved = flux(there, component)
    for c in range(5):
        term = wave * (there[c] - here[c])
        term = term - moved[c] if sign > 0 else term + moved[c]
        total[c] = term if total[c] is None else total[c] + term


def kernel(
    shift,
    sectors,
    offset_ref,
    wheel_ref,
    state_ref,
    volume_ref,
    new_ref,
    rate_ref,
    cells0,
    cells1,
    packed,
    ghosts,
    edges,
    rows,
    layer_out,
    layer_in,
    rest_out,
    rest_in,
    other_part,
    send_sem,
    recv_sem,
    far_send,
    far_recv,
):
    row = lax.axis_index("row")
    sector = lax.axis_index("circ")
    rad = lax.axis_index("rad")
    layers, height, width = state_ref.shape[2:]
    tall = height // PARTS
    tiles = PARTS
    left = {"circ": lax.rem(sector + sectors - 1, sectors)}
    right = {"circ": lax.rem(sector + 1, sectors)}
    beside = {"rad": 1 - rad}
    near = lax.rem(sector + jnp.where(row == 0, shift, sectors - shift), sectors)
    after = lax.rem(near + jnp.where(row == 0, 1, sectors - 1), sectors)
    facing = [{"row": 1 - row, "circ": near}, {"row": 1 - row, "circ": after}]

    barrier = pltpu.get_barrier_semaphore()
    for device in [left, right, beside] + facing:
        pl.semaphore_signal(barrier, inc=1, device_id=device, device_id_type=MESH)

    sigma = (1 - 2 * row).astype(jnp.float32)
    face_layer = jnp.where(row == 0, layers - 1, 0)
    lanes = lax.broadcasted_iota(jnp.int32, (tall, width), 1)
    inner_row = PAD + jnp.where(rad == 0, height - 1, 0)
    inner_pad = PAD + jnp.where(rad == 0, height, -1)
    wall_row = PAD + jnp.where(rad == 0, 0, height - 1)
    wall_pad = PAD + jnp.where(rad == 0, -1, height)
    diagonal = lax.broadcasted_iota(jnp.int32, (height, height), 0) == lax.broadcasted_iota(
        jnp.int32, (height, height), 1
    )
    wheel = jnp.sum(
        jnp.where(diagonal, jnp.broadcast_to(wheel_ref[...], (height, height)), 0.0),
        axis=1,
        keepdims=True,
    )
    rest = lax.rem(offset_ref[0], width)
    turn = jnp.where(row == 0, lax.rem(width - rest, width), rest)
    low_lanes = lanes < jnp.where(row == 0, width - rest, rest)

    def span(t, by=0):
        return pl.ds(PAD + tall * t + by, tall)

    def layer_at(i):
        return jnp.where(row == 0, layers - 1 - i, i)

    def other_frame(u, t):
        speed = sigma * wheel[tall * t : tall * t + tall]
        return [
            u[0],
            u[1],
            u[2],
            u[3] + u[0] * speed,
            u[4] + u[3] * speed + 0.5 * u[0] * speed * speed,
        ]

    def keep(cells, round_, a, t, u):
        values = quantities(u)
        for q in range(QUANTITIES):
            cells[q, a, span(t), :] = values[q]
        first = jnp.zeros((tall, width), jnp.float32)
        last = first
        for i, q in enumerate(CIRCUM):
            here = lanes == 8 * i
            first = jnp.where(here, pltpu.roll(values[q], 8 * i, 1) if i else values[q], first)
            last = jnp.where(here, pltpu.roll(values[q], 8 * i + 1, 1), last)
        here = lax.rem(lanes, 8) == a
        for side, tile in ((0, first), (1, last)):
            at = (round_, side, pl.ds(tall * t, tall), slice(None))
            packed[at] = jnp.where(here, pltpu.roll(tile, a, 1), packed[at])

    def keep_rows(cells, round_, a):
        for i, q in enumerate(RADIAL):
            rows[round_, i, pl.ds(a, 1), :] = cells[q, a, pl.ds(inner_row, 1), :]
            wall = cells[q, a, pl.ds(wall_row, 1), :]
            cells[q, a, pl.ds(wall_pad, 1), :] = -wall if q in (2, V2) else wall

    def rate_of(cells, round_, a, t):
        def tile(qs, layer, by=0):
            return [cells[q, layer, span(t, by), :] for q in qs]

        total = [None] * 5
        here = tile(AXIAL, a)
        add_side(total, here, tile(AXIAL, jnp.minimum(a + 1, layers - 1)), 1, 1)
        add_side(total, here, tile(AXIAL, jnp.maximum(a - 1, 0)), 1, -1)
        here = tile(RADIAL, a)
        add_side(total, here, tile(RADIAL, a, 1), 2, 1)
        add_side(total, here, tile(RADIAL, a, -1), 2, -1)
        here = tile(CIRCUM, a)
        at = pl.ds(tall * t, tall)
        before = pltpu.roll(ghosts[round_, 0, at, :], lax.rem(width - a, width), 1)
        after_ = pltpu.roll(ghosts[round_, 1, at, :], width - 1 - a, 1)
        above, below = [], []
        for i in range(8):
            ghost = pltpu.roll(after_, width - 8 * i, 1) if i else after_
            above.append(jnp.where(lanes == width - 1, ghost, pltpu.roll(here[i], width - 1, 1)))
            ghost = pltpu.roll(before, width - 8 * i, 1) if i else before
            below.append(jnp.where(lanes == 0, ghost, pltpu.roll(here[i], 1, 1)))
        add_side(total, here, above, 3, 1)
        add_side(total, here, below, 3, -1)
        half = 0.5 * volume_ref[0, a, pl.ds(tall * t, tall), :]
        return [half * part for part in total]

    def place_rows(cells, round_, a):
        for i, q in enumerate(RADIAL):
            cells[q, a, pl.ds(inner_pad, 1), :] = edges[round_, i, pl.ds(a, 1), :]

    def local_copies(round_):
        return [
            pltpu.make_async_remote_copy(
                src_ref=src,
                dst_ref=dst,
                send_sem=send_sem.at[round_, i],
                recv_sem=recv_sem.at[round_, i],
                device_id=device,
                device_id_type=MESH,
            )
            for i, (src, dst, device) in enumerate(
                (
                    (packed.at[round_, 0], ghosts.at[round_, 1], left),
                    (packed.at[round_, 1], ghosts.at[round_, 0], right),
                    (rows.at[round_], edges.at[round_], beside),
                )
            )
        ]

    def far_copies(which, src, dst):
        return [
            pltpu.make_async_remote_copy(
                src_ref=src,
                dst_ref=dst.at[i],
                send_sem=far_send.at[which, i],
                recv_sem=far_recv.at[which, i],
                device_id=facing[i],
                device_id_type=MESH,
            )
            for i in range(2)
        ]

    def window(arrived, c, t):
        at = pl.ds(tall * t, tall)
        return jnp.where(
            low_lanes,
            pltpu.roll(arrived[row, c, at, :], turn, 1),
            pltpu.roll(arrived[1 - row, c, at, :], turn, 1),
        )

    def face_terms(mine, other):
        own, theirs = flux(mine, 1), flux(other, 1)
        wave = jnp.maximum(jnp.abs(mine[5]) + mine[7], jnp.abs(other[5]) + other[7])
        turned = [sigma * (own[c] - theirs[c]) for c in range(5)]
        spread = [wave * (other[c] - mine[c]) for c in range(5)]
        return turned, spread

    def start(copies):
        for copy in copies:
            copy.start()

    local = [local_copies(r) for r in range(3)]
    far_layer = far_copies(0, layer_out, layer_in)
    far_rest = far_copies(1, rest_out, rest_in)

    for r in range(3):
        packed[r] = jnp.zeros_like(packed[r])

    def prepare(a, carry):
        for t in range(tiles):
            keep(cells0, 0, a, t, [state_ref[0, c, a, pl.ds(tall * t, tall), :] for c in range(5)])
        keep_rows(cells0, 0, a)
        return carry

    lax.fori_loop(0, layers, prepare, 0)
    for t in range(tiles):
        at = pl.ds(tall * t, tall)
        moved = other_frame([state_ref[0, c, face_layer, at, :] for c in range(5)], t)
        for c in range(5):
            layer_out[c, at, :] = moved[c]
        layer_out[5, at, :] = volume_ref[0, face_layer, at, :]

    pl.semaphore_wait(barrier, 5)
    start(local[0])
    start(far_layer)
    for copy in local[0]:
        copy.wait_recv()

    def first_section(i, carry):
        a = layer_at(i)
        place_rows(cells0, 0, a)
        for t in range(tiles):
            rate = rate_of(cells0, 0, a, t)
            u = [cells0[c, a, span(t), :] + TIME_STEP * rate[c] for c in range(5)]
            keep(cells1, 1, a, t, u)
        keep_rows(cells1, 1, a)

        @pl.when(i == 0)
        def _():
            for t in range(tiles):
                moved = other_frame([cells1[c, a, span(t), :] for c in range(5)], t)
                for c in range(5):
                    rest_out[c, pl.ds(tall * t, tall), :] = moved[c]
            start(far_rest)

        return carry

    lax.fori_loop(0, layers, first_section, 0)
    start(local[1])
    for copy in local[1]:
        copy.wait_recv()

    def interface_first():
        for copy in far_layer:
            copy.wait_recv()
        a = face_layer
        for t in range(tiles):
            at = pl.ds(tall * t, tall)
            theirs = quantities([window(layer_in, c, t) for c in range(5)])
            mine = [cells0[q, a, span(t), :] for q in AXIAL]
            turned, spread = face_terms(mine, [theirs[q] for q in AXIAL])
            scale = (0.5 * TIME_STEP) * volume_ref[0, a, at, :]
            other_scale = (0.5 * TIME_STEP) * window(layer_in, 5, t)
            u = []
            for c in range(5):
                other_part[c, at, :] = other_scale * (turned[c] - spread[c])
                u.append(cells1[c, a, span(t), :] + scale * (turned[c] + spread[c]))
            keep(cells1, 2, a, t, u)
        keep_rows(cells1, 2, a)
        start(local[2])

    def second_section(j, carry):
        i = layers - 1 - j
        a = layer_at(i)
        round_ = jnp.where(i == 0, 2, 1)
        pl.when(i == 1)(interface_first)

        @pl.when(i == 0)
        def _():
            for copy in local[2]:
                copy.wait_recv()

        place_rows(cells1, round_, a)
        for t in range(tiles):
            at = pl.ds(tall * t, tall)
            rate = rate_of(cells1, round_, a, t)
            for c in range(5):
                rate_ref[0, c, a, at, :] = rate[c]
                new_ref[0, c, a, at, :] = 0.5 * cells0[c, a, span(t), :] + 0.5 * (
                    cells1[c, a, span(t), :] + TIME_STEP * rate[c]
                )
        return carry

    lax.fori_loop(0, layers, second_section, 0)
    for copy in far_rest:
        copy.wait_recv()
    a = face_layer
    for t in range(tiles):
        at = pl.ds(tall * t, tall)
        theirs = quantities(
            [window(rest_in, c, t) + other_part[c, at, :] for c in range(5)]
        )
        mine = [cells1[q, a, span(t), :] for q in AXIAL]
        turned, spread = face_terms(mine, [theirs[q] for q in AXIAL])
        half = 0.5 * volume_ref[0, a, at, :]
        for c in range(5):
            gain = half * (turned[c] + spread[c])
            rate_ref[0, c, a, at, :] += gain
            new_ref[0, c, a, at, :] += (0.5 * TIME_STEP) * gain
    for copy in local[0] + local[1] + local[2] + far_layer + far_rest:
        copy.wait_send()


def step(shift, state, inv_volume, wheel, offset):
    sectors = lax.axis_size("circ")
    layers, height, width = state.shape[2:]
    f32 = jnp.float32
    cells = pltpu.VMEM((QUANTITIES, layers, height + 2 * PAD, width), f32)
    vmem = pl.BlockSpec(memory_space=pltpu.VMEM)
    out = jax.ShapeDtypeStruct(state.shape, f32)
    return pl.pallas_call(
        functools.partial(kernel, shift, sectors),
        out_shape=(out, out),
        in_specs=[pl.BlockSpec(memory_space=pltpu.SMEM), vmem, vmem, vmem],
        out_specs=(vmem, vmem),
        scratch_shapes=[
            cells,
            cells,
            pltpu.VMEM((3, 2, height, width), f32),
            pltpu.VMEM((3, 2, height, width), f32),
            pltpu.VMEM((3, 8, layers, width), f32),
            pltpu.VMEM((3, 8, layers, width), f32),
            pltpu.VMEM((6, height, width), f32),
            pltpu.VMEM((2, 6, height, width), f32),
            pltpu.VMEM((5, height, width), f32),
            pltpu.VMEM((2, 5, height, width), f32),
            pltpu.VMEM((5, height, width), f32),
            pltpu.SemaphoreType.DMA((3, 3)),
            pltpu.SemaphoreType.DMA((3, 3)),
            pltpu.SemaphoreType.DMA((2, 2)),
            pltpu.SemaphoreType.DMA((2, 2)),
        ],
        compiler_params=pltpu.CompilerParams(
            collective_id=shift, has_side_effects=True, vmem_limit_bytes=32 * 2**20
        ),
    )(offset, wheel[None, :], state, inv_volume)


def on_device(state, inv_volume, wheel_speed, offset):
    return lax.switch(
        offset[0] // state.shape[4],
        [functools.partial(step, shift) for shift in range(lax.axis_size("circ"))],
        state,
        inv_volume,
        wheel_speed,
        offset,
    )


def solution(mesh):
    return jax.shard_map(
        on_device,
        mesh=mesh,
        in_specs=(
            P("row", None, None, "rad", "circ"),
            P("row", None, "rad", "circ"),
            P("rad"),
            P(),
        ),
        out_specs=(P("row", None, None, "rad", "circ"), P("row", None, None, "rad", "circ")),
        check_vma=False,
    )
```

```python
import functools

import jax
import jax.numpy as jnp
from jax import lax
from jax.experimental import pallas as pl
from jax.experimental.pallas import tpu as pltpu
from jax.sharding import PartitionSpec as P

GAMMA = 1.4
TIME_STEP = 0.05
MESH = pl.DeviceIdType.MESH

V1, V2, V3, PRESSURE, SOUND = 5, 6, 7, 8, 9
QUANTITIES = 10
AXIAL = (0, 1, 2, 3, 4, V1, PRESSURE, SOUND)
RADIAL = (0, 1, 2, 3, 4, V2, PRESSURE, SOUND)
CIRCUM = (0, 1, 2, 3, 4, V3, PRESSURE, SOUND)
PAD = 8
GHOST, OTHER, BEYOND, FACING = 8, 9, 10, 11
SLOTS = 16


def quantities(u):
    inverse = 1.0 / u[0]
    v1, v2, v3 = u[1] * inverse, u[2] * inverse, u[3] * inverse
    pressure = (GAMMA - 1.0) * (u[4] - 0.5 * (u[1] * v1 + u[2] * v2 + u[3] * v3))
    return list(u) + [v1, v2, v3, pressure, jnp.sqrt(GAMMA * pressure * inverse)]


def flux(cell, component):
    speed, pressure = cell[5], cell[6]
    out = [cell[c] * speed for c in range(4)] + [(cell[4] + pressure) * speed]
    out[component] = out[component] + pressure
    return out


def add_side(total, here, there, component, sign):
    wave = jnp.maximum(jnp.abs(here[5]) + here[7], jnp.abs(there[5]) + there[7])
    moved = flux(there, component)
    for c in range(5):
        term = wave * (there[c] - here[c])
        term = term - moved[c] if sign > 0 else term + moved[c]
        total[c] = term if total[c] is None else total[c] + term


def far_kernel(shift, sectors, state_ref, volume_ref, got_ref, send_sem, recv_sem):
    row = lax.axis_index("row")
    sector = lax.axis_index("circ")
    layers = state_ref.shape[2]
    near = lax.rem(sector + jnp.where(row == 0, shift, sectors - shift), sectors)
    after = lax.rem(near + jnp.where(row == 0, 1, sectors - 1), sectors)
    targets = [{"row": 1 - row, "circ": near}, {"row": 1 - row, "circ": after}]
    barrier = pltpu.get_barrier_semaphore()
    for target in targets:
        pl.semaphore_signal(barrier, inc=1, device_id=target, device_id_type=MESH)
    pl.semaphore_wait(barrier, 2)
    outer = jnp.where(row == 0, layers - 1, 0)
    inner = jnp.where(row == 0, layers - 2, 1)
    copies = []
    for j, (src, at) in enumerate(
        (
            (state_ref.at[0, :, outer], pl.ds(0, 5)),
            (state_ref.at[0, :, inner], pl.ds(5, 5)),
            (volume_ref.at[:, outer], pl.ds(10, 1)),
        )
    ):
        for i in range(2):
            copies.append(
                pltpu.make_async_remote_copy(
                    src_ref=src,
                    dst_ref=got_ref.at[i, at],
                    send_sem=send_sem.at[j, i],
                    recv_sem=recv_sem.at[j, i],
                    device_id=targets[i],
                    device_id_type=MESH,
                )
            )
    for copy in copies:
        copy.start()
    for copy in copies:
        copy.wait()


def kernel(
    sectors,
    offset_ref,
    wheel_ref,
    state_ref,
    volume_ref,
    far_ref,
    new_ref,
    rate_ref,
    cells0,
    cells1,
    volumes,
    packed,
    ghosts,
    edges,
    rows,
    send_sem,
    recv_sem,
):
    row = lax.axis_index("row")
    sector = lax.axis_index("circ")
    rad = lax.axis_index("rad")
    layers, height, width = state_ref.shape[2:]
    left = {"circ": lax.rem(sector + sectors - 1, sectors)}
    right = {"circ": lax.rem(sector + 1, sectors)}
    beside = {"rad": 1 - rad}
    barrier = pltpu.get_barrier_semaphore()
    for device in (left, right, beside):
        pl.semaphore_signal(barrier, inc=1, device_id=device, device_id_type=MESH)

    sigma = (1 - 2 * row).astype(jnp.float32)
    face_layer = jnp.where(row == 0, layers - 1, 0)
    lanes = lax.broadcasted_iota(jnp.int32, (height, width), 1)
    inner_row = PAD + jnp.where(rad == 0, height - 1, 0)
    inner_pad = PAD + jnp.where(rad == 0, height, -1)
    wall_row = PAD + jnp.where(rad == 0, 0, height - 1)
    wall_pad = PAD + jnp.where(rad == 0, -1, height)
    diagonal = lax.broadcasted_iota(jnp.int32, (height, height), 0) == lax.broadcasted_iota(
        jnp.int32, (height, height), 1
    )
    wheel = jnp.sum(
        jnp.where(diagonal, jnp.broadcast_to(wheel_ref[...], (height, height)), 0.0),
        axis=1,
        keepdims=True,
    )
    rest = lax.rem(offset_ref[0], width)
    turn = jnp.where(row == 0, lax.rem(width - rest, width), rest)
    low_lanes = lanes < jnp.where(row == 0, width - rest, rest)
    body = pl.ds(PAD, height)

    def other_frame(u, speed):
        return [
            u[0],
            u[1],
            u[2],
            u[3] + u[0] * speed,
            u[4] + u[3] * speed + 0.5 * u[0] * speed * speed,
        ]

    def window(c):
        return jnp.where(
            low_lanes,
            pltpu.roll(far_ref[row, c], turn, 1),
            pltpu.roll(far_ref[1 - row, c], turn, 1),
        )

    def keep(cells, a, u):
        values = quantities(u)
        for q in range(QUANTITIES):
            cells[q, a, body, :] = values[q]
        return values

    def pack(round_, a, values):
        first = jnp.zeros((height, width), jnp.float32)
        last = first
        for i, q in enumerate(CIRCUM):
            here = lanes == SLOTS * i
            x = values[q]
            first = jnp.where(here, pltpu.roll(x, SLOTS * i, 1) if i else x, first)
            last = jnp.where(here, pltpu.roll(x, SLOTS * i + 1, 1), last)
        here = lax.rem(lanes, SLOTS) == a
        for side, tile in ((0, first), (1, last)):
            packed[round_, side] = jnp.where(here, pltpu.roll(tile, a, 1), packed[round_, side])

    def keep_rows(cells, round_, a):
        for i, q in enumerate(RADIAL):
            rows[round_, i, pl.ds(a, 1), :] = cells[q, a, pl.ds(inner_row, 1), :]
            wall = cells[q, a, pl.ds(wall_row, 1), :]
            cells[q, a, pl.ds(wall_pad, 1), :] = -wall if q in (2, V2) else wall

    def rate_of(cells, round_, i):
        a = jnp.where(i == layers, OTHER, i)
        below = jnp.where(row == 0, jnp.maximum(i - 1, 0), jnp.where(i == 0, GHOST, i - 1))
        below = jnp.where(i == layers, jnp.where(row == 0, FACING, BEYOND), below)
        above = jnp.where(row == 0, i + 1, jnp.minimum(i + 1, layers - 1))
        above = jnp.where(i == layers, jnp.where(row == 0, BEYOND, FACING), above)
        for j, q in enumerate(RADIAL):
            cells[q, a, pl.ds(inner_pad, 1), :] = edges[round_, j, pl.ds(a, 1), :]

        def layer(qs, slot, by=0):
            return [cells[q, slot, pl.ds(PAD + by, height), :] for q in qs]

        total = [None] * 5
        here = layer(AXIAL, a)
        add_side(total, here, layer(AXIAL, above), 1, 1)
        add_side(total, here, layer(AXIAL, below), 1, -1)
        here = layer(RADIAL, a)
        add_side(total, here, layer(RADIAL, a, 1), 2, 1)
        add_side(total, here, layer(RADIAL, a, -1), 2, -1)
        here = layer(CIRCUM, a)
        before = pltpu.roll(ghosts[round_, 0], lax.rem(width - a, width), 1)
        after = pltpu.roll(ghosts[round_, 1], width - 1 - a, 1)
        up, down = [], []
        for j in range(8):
            ghost = pltpu.roll(after, width - SLOTS * j, 1) if j else after
            up.append(jnp.where(lanes == width - 1, ghost, pltpu.roll(here[j], width - 1, 1)))
            ghost = pltpu.roll(before, width - SLOTS * j, 1) if j else before
            down.append(jnp.where(lanes == 0, ghost, pltpu.roll(here[j], 1, 1)))
        add_side(total, here, up, 3, 1)
        add_side(total, here, down, 3, -1)
        half = 0.5 * volumes[i]
        return a, [half * part for part in total]

    def local_copies(round_):
        return [
            pltpu.make_async_remote_copy(
                src_ref=src,
                dst_ref=dst,
                send_sem=send_sem.at[round_, i],
                recv_sem=recv_sem.at[round_, i],
                device_id=device,
                device_id_type=MESH,
            )
            for i, (src, dst, device) in enumerate(
                (
                    (packed.at[round_, 0], ghosts.at[round_, 1], left),
                    (packed.at[round_, 1], ghosts.at[round_, 0], right),
                    (rows.at[round_], edges.at[round_], beside),
                )
            )
        ]

    def send(copies):
        for copy in copies:
            copy.start()
        for copy in copies:
            copy.wait_recv()

    local = [local_copies(r) for r in range(2)]
    for r in range(2):
        packed[r] = jnp.zeros_like(packed[r])
        rows[r] = jnp.zeros_like(rows[r])

    def prepare(a, carry):
        pack(0, a, keep(cells0, a, [state_ref[0, c, a] for c in range(5)]))
        keep_rows(cells0, 0, a)
        volumes[a] = volume_ref[0, a]
        return carry

    lax.fori_loop(0, layers, prepare, 0)
    other = [window(c) for c in range(5)]
    pack(0, OTHER, keep(cells0, OTHER, other))
    keep_rows(cells0, 0, OTHER)
    keep(cells0, GHOST, other_frame(other, -sigma * wheel))
    volumes[layers] = window(10)

    pl.semaphore_wait(barrier, 3)
    for copy in local[0]:
        copy.start()
    keep(cells0, BEYOND, [window(5 + c) for c in range(5)])
    mine = [state_ref[0, c, face_layer] for c in range(5)]
    keep(cells0, FACING, other_frame(mine, sigma * wheel))
    for copy in local[0]:
        copy.wait_recv()

    def first_section(i, carry):
        a, rate = rate_of(cells0, 0, i)
        u = [cells0[c, a, body, :] + TIME_STEP * rate[c] for c in range(5)]
        turned = jnp.where(i == layers, -sigma, 0.0) * wheel
        pack(1, i, keep(cells1, i, other_frame(u, turned)))
        keep_rows(cells1, 1, i)
        return carry

    lax.fori_loop(0, layers + 1, first_section, 0)
    send(local[1])

    def second_section(i, carry):
        _, rate = rate_of(cells1, 1, i)
        for c in range(5):
            rate_ref[0, c, i] = rate[c]
            new_ref[0, c, i] = 0.5 * cells0[c, i, body, :] + 0.5 * (
                cells1[c, i, body, :] + TIME_STEP * rate[c]
            )
        return carry

    lax.fori_loop(0, layers, second_section, 0)
    for copy in local[0] + local[1]:
        copy.wait_send()


def far(shift, state, inv_volume):
    height, width = state.shape[3:]
    anywhere = pl.BlockSpec(memory_space=pl.ANY)
    return pl.pallas_call(
        functools.partial(far_kernel, shift, lax.axis_size("circ")),
        out_shape=jax.ShapeDtypeStruct((2, 11, height, width), jnp.float32),
        in_specs=[anywhere, anywhere],
        out_specs=anywhere,
        scratch_shapes=[pltpu.SemaphoreType.DMA((3, 2)), pltpu.SemaphoreType.DMA((3, 2))],
        compiler_params=pltpu.CompilerParams(collective_id=shift, has_side_effects=True),
    )(state, inv_volume)


def on_device(state, inv_volume, wheel_speed, offset):
    sectors = lax.axis_size("circ")
    layers, height, width = state.shape[2:]
    arrived = lax.switch(
        offset[0] // width,
        [functools.partial(far, shift) for shift in range(sectors)],
        state,
        inv_volume,
    )
    f32 = jnp.float32
    cells = pltpu.VMEM((QUANTITIES, layers + 4, height + 2 * PAD, width), f32)
    vmem = pl.BlockSpec(memory_space=pltpu.VMEM)
    out = jax.ShapeDtypeStruct(state.shape, f32)
    return pl.pallas_call(
        functools.partial(kernel, sectors),
        out_shape=(out, out),
        in_specs=[pl.BlockSpec(memory_space=pltpu.SMEM)] + [vmem] * 4,
        out_specs=(vmem, vmem),
        scratch_shapes=[
            cells,
            cells,
            pltpu.VMEM((layers + 1, height, width), f32),
            pltpu.VMEM((2, 2, height, width), f32),
            pltpu.VMEM((2, 2, height, width), f32),
            pltpu.VMEM((2, 8, SLOTS, width), f32),
            pltpu.VMEM((2, 8, SLOTS, width), f32),
            pltpu.SemaphoreType.DMA((2, 3)),
            pltpu.SemaphoreType.DMA((2, 3)),
        ],
        compiler_params=pltpu.CompilerParams(
            collective_id=sectors, has_side_effects=True, vmem_limit_bytes=32 * 2**20
        ),
    )(offset, wheel_speed[None, :], state, inv_volume, arrived)


def solution(mesh):
    return jax.shard_map(
        on_device,
        mesh=mesh,
        in_specs=(
            P("row", None, None, "rad", "circ"),
            P("row", None, "rad", "circ"),
            P("rad"),
            P(),
        ),
        out_specs=(P("row", None, None, "rad", "circ"), P("row", None, None, "rad", "circ")),
        check_vma=False,
    )
```

```python
import functools

import jax
import jax.numpy as jnp
from jax import lax
from jax.experimental import pallas as pl
from jax.experimental.pallas import tpu as pltpu
from jax.sharding import PartitionSpec as P

GAMMA = 1.4
TIME_STEP = 0.05
MESH = pl.DeviceIdType.MESH

V1, V2, V3, PRESSURE, SOUND = 5, 6, 7, 8, 9
QUANTITIES = 10
AXIAL = (0, 1, 2, 3, 4, V1, PRESSURE, SOUND)
RADIAL = (0, 1, 2, 3, 4, V2, PRESSURE, SOUND)
CIRCUM = (0, 1, 2, 3, 4, V3, PRESSURE, SOUND)
PAD = 8
GHOST, OTHER, BEYOND, FACING = 8, 9, 10, 11
SPARE = 12
SLOTS = 16


def quantities(u):
    inverse = 1.0 / u[0]
    v1, v2, v3 = u[1] * inverse, u[2] * inverse, u[3] * inverse
    pressure = (GAMMA - 1.0) * (u[4] - 0.5 * (u[1] * v1 + u[2] * v2 + u[3] * v3))
    return list(u) + [v1, v2, v3, pressure, jnp.sqrt(GAMMA * pressure * inverse)]


def flux(cell, component):
    speed, pressure = cell[5], cell[6]
    out = [cell[c] * speed for c in range(4)] + [(cell[4] + pressure) * speed]
    out[component] = out[component] + pressure
    return out


def add_side(total, here, there, component, sign):
    wave = jnp.maximum(jnp.abs(here[5]) + here[7], jnp.abs(there[5]) + there[7])
    moved = flux(there, component)
    for c in range(5):
        term = wave * (there[c] - here[c])
        term = term - moved[c] if sign > 0 else term + moved[c]
        total[c] = term if total[c] is None else total[c] + term


def far_kernel(shift, sectors, state_ref, volume_ref, got_ref, send_sem, recv_sem):
    row = lax.axis_index("row")
    sector = lax.axis_index("circ")
    layers = state_ref.shape[2]
    near = lax.rem(sector + jnp.where(row == 0, shift, sectors - shift), sectors)
    target = {"row": 1 - row, "circ": near}
    barrier = pltpu.get_barrier_semaphore()
    pl.semaphore_signal(barrier, inc=1, device_id=target, device_id_type=MESH)
    pl.semaphore_wait(barrier, 1)
    outer = jnp.where(row == 0, layers - 1, 0)
    inner = jnp.where(row == 0, layers - 2, 1)
    copies = []
    for j, (src, at) in enumerate(
        (
            (state_ref.at[0, :, outer], pl.ds(0, 5)),
            (state_ref.at[0, :, inner], pl.ds(5, 5)),
            (volume_ref.at[:, outer], pl.ds(10, 1)),
        )
    ):
        copies.append(
            pltpu.make_async_remote_copy(
                src_ref=src,
                dst_ref=got_ref.at[at],
                send_sem=send_sem.at[j],
                recv_sem=recv_sem.at[j],
                device_id=target,
                device_id_type=MESH,
            )
        )
    for copy in copies:
        copy.start()
    for copy in copies:
        copy.wait()


def kernel(
    sectors,
    offset_ref,
    wheel_ref,
    state_ref,
    volume_ref,
    far_ref,
    new_ref,
    rate_ref,
    cells0,
    cells1,
    volumes,
    packed,
    ghosts,
    edges,
    rows,
    halves_out,
    halves_in,
    send_sem,
    recv_sem,
):
    row = lax.axis_index("row")
    sector = lax.axis_index("circ")
    rad = lax.axis_index("rad")
    layers, height, width = state_ref.shape[2:]
    left = {"circ": lax.rem(sector + sectors - 1, sectors)}
    right = {"circ": lax.rem(sector + 1, sectors)}
    beside = {"rad": 1 - rad}
    barrier = pltpu.get_barrier_semaphore()
    for device in (left, right, beside):
        pl.semaphore_signal(barrier, inc=1, device_id=device, device_id_type=MESH)

    sigma = (1 - 2 * row).astype(jnp.float32)
    face_layer = jnp.where(row == 0, layers - 1, 0)
    lanes = lax.broadcasted_iota(jnp.int32, (height, width), 1)
    inner_row = PAD + jnp.where(rad == 0, height - 1, 0)
    inner_pad = PAD + jnp.where(rad == 0, height, -1)
    wall_row = PAD + jnp.where(rad == 0, 0, height - 1)
    wall_pad = PAD + jnp.where(rad == 0, -1, height)
    diagonal = lax.broadcasted_iota(jnp.int32, (height, height), 0) == lax.broadcasted_iota(
        jnp.int32, (height, height), 1
    )
    wheel = jnp.sum(
        jnp.where(diagonal, jnp.broadcast_to(wheel_ref[...], (height, height)), 0.0),
        axis=1,
        keepdims=True,
    )
    rest = lax.rem(offset_ref[0] + width // 2, width)
    turn = jnp.where(row == 0, lax.rem(width - rest, width), rest)
    low_lanes = lanes < jnp.where(row == 0, width - rest, rest)
    body = pl.ds(PAD, height)

    def other_frame(u, speed):
        return [
            u[0],
            u[1],
            u[2],
            u[3] + u[0] * speed,
            u[4] + u[3] * speed + 0.5 * u[0] * speed * speed,
        ]

    half_width, half_height = width // 2, height // 2
    low_half = lanes < half_width
    low_top = lanes[:half_height] < half_width

    def split(c):
        top, bottom = far_ref[c, :half_height], far_ref[c, half_height:]
        halves_out[0, c] = jnp.where(low_top, top, pltpu.roll(bottom, half_width, 1))
        halves_out[1, c] = jnp.where(low_top, pltpu.roll(top, half_width, 1), bottom)

    def turned(c):
        middle = pltpu.roll(far_ref[c], half_width, 1)
        late, early = halves_in[0, c], halves_in[1, c]
        before = jnp.concatenate([early, pltpu.roll(early, half_width, 1)])
        after = jnp.concatenate([pltpu.roll(late, half_width, 1), late])
        return (
            pltpu.roll(jnp.where(low_half, before, middle), turn, 1),
            pltpu.roll(jnp.where(low_half, middle, after), turn, 1),
        )

    def window(c):
        low, high = turned(c)
        return jnp.where(low_lanes, low, high)

    def keep(cells, a, u):
        values = quantities(u)
        for q in range(QUANTITIES):
            cells[q, a, body, :] = values[q]
        return values

    def columns(a, firsts, lasts):
        first = jnp.zeros((height, width), jnp.float32)
        last = first
        for i, q in enumerate(CIRCUM):
            here = lanes == SLOTS * i
            x = firsts[q]
            first = jnp.where(here, pltpu.roll(x, SLOTS * i, 1) if i else x, first)
            last = jnp.where(here, pltpu.roll(lasts[q], SLOTS * i + 1, 1), last)
        return pltpu.roll(first, a, 1), pltpu.roll(last, a, 1)

    def pack(round_, a, values):
        here = lax.rem(lanes, SLOTS) == a
        for side, tile in enumerate(columns(a, values, values)):
            packed[round_, side] = jnp.where(here, tile, packed[round_, side])

    def keep_rows(cells, round_, a):
        for i, q in enumerate(RADIAL):
            rows[round_, i, pl.ds(a, 1), :] = cells[q, a, pl.ds(inner_row, 1), :]
            wall = cells[q, a, pl.ds(wall_row, 1), :]
            cells[q, a, pl.ds(wall_pad, 1), :] = -wall if q in (2, V2) else wall

    def rate_of(cells, round_, i):
        a = jnp.where(i == layers, OTHER, i)
        below = jnp.where(row == 0, jnp.maximum(i - 1, 0), jnp.where(i == 0, GHOST, i - 1))
        below = jnp.where(i == layers, jnp.where(row == 0, FACING, BEYOND), below)
        above = jnp.where(row == 0, i + 1, jnp.minimum(i + 1, layers - 1))
        above = jnp.where(i == layers, jnp.where(row == 0, BEYOND, FACING), above)
        for j, q in enumerate(RADIAL):
            cells[q, a, pl.ds(inner_pad, 1), :] = edges[round_, j, pl.ds(a, 1), :]

        def layer(qs, slot, by=0):
            return [cells[q, slot, pl.ds(PAD + by, height), :] for q in qs]

        total = [None] * 5
        here = layer(AXIAL, a)
        add_side(total, here, layer(AXIAL, above), 1, 1)
        add_side(total, here, layer(AXIAL, below), 1, -1)
        here = layer(RADIAL, a)
        add_side(total, here, layer(RADIAL, a, 1), 2, 1)
        add_side(total, here, layer(RADIAL, a, -1), 2, -1)
        here = layer(CIRCUM, a)
        before = pltpu.roll(ghosts[round_, 0], lax.rem(width - a, width), 1)
        after = pltpu.roll(ghosts[round_, 1], width - 1 - a, 1)
        up, down = [], []
        for j in range(8):
            ghost = pltpu.roll(after, width - SLOTS * j, 1) if j else after
            up.append(jnp.where(lanes == width - 1, ghost, pltpu.roll(here[j], width - 1, 1)))
            ghost = pltpu.roll(before, width - SLOTS * j, 1) if j else before
            down.append(jnp.where(lanes == 0, ghost, pltpu.roll(here[j], 1, 1)))
        add_side(total, here, up, 3, 1)
        add_side(total, here, down, 3, -1)
        half = 0.5 * volumes[i]
        return a, [half * part for part in total]

    def local_copies(round_):
        return [
            pltpu.make_async_remote_copy(
                src_ref=src,
                dst_ref=dst,
                send_sem=send_sem.at[round_, i],
                recv_sem=recv_sem.at[round_, i],
                device_id=device,
                device_id_type=MESH,
            )
            for i, (src, dst, device) in enumerate(
                (
                    (packed.at[round_, 0], ghosts.at[round_, 1], left),
                    (packed.at[round_, 1], ghosts.at[round_, 0], right),
                    (rows.at[round_, :, pl.ds(0, 8)], edges.at[round_, :, pl.ds(0, 8)], beside),
                    (halves_out.at[0], halves_in.at[0], left),
                    (halves_out.at[1], halves_in.at[1], right),
                    (rows.at[round_, :, pl.ds(8, 8)], edges.at[round_, :, pl.ds(8, 8)], beside),
                )
            )
            if round_ == 0 or i < 3
        ]

    def send(copies):
        for copy in copies:
            copy.start()
        for copy in copies:
            copy.wait_recv()

    local = [local_copies(r) for r in range(2)]
    for r in range(2):
        packed[r] = jnp.zeros_like(packed[r])
        rows[r] = jnp.zeros_like(rows[r])

    def prepare(a, carry):
        pack(0, a, keep(cells0, a, [state_ref[0, c, a] for c in range(5)]))
        keep_rows(cells0, 0, a)
        volumes[a] = volume_ref[0, a]
        return carry

    lax.fori_loop(0, layers, prepare, 0)
    for c in range(11):
        split(c)
    middle = [pltpu.roll(far_ref[c], half_width, 1) for c in range(5)]
    pack(0, SPARE, quantities(middle))

    pl.semaphore_wait(barrier, 3)
    for copy in local[0][:5]:
        copy.start()
    mine = [state_ref[0, c, face_layer] for c in range(5)]
    keep(cells0, FACING, other_frame(mine, sigma * wheel))
    for copy in local[0][:5]:
        copy.wait_recv()

    pairs = [turned(c) for c in range(5)]
    other = [jnp.where(low_lanes, low, high) for low, high in pairs]
    keep(cells0, OTHER, other)
    keep_rows(cells0, 0, OTHER)
    local[0][5].start()
    keep(cells0, GHOST, other_frame(other, -sigma * wheel))
    keep(cells0, BEYOND, [window(5 + c) for c in range(5)])
    volumes[layers] = window(10)
    late, early = columns(
        OTHER, quantities([high for _, high in pairs]), quantities([low for low, _ in pairs])
    )
    begin = jnp.where(row == 0, rest, width - rest)
    here = lax.rem(lanes, SLOTS) == OTHER
    for side, tile, edge in ((0, early, 0), (1, late, width)):
        got = ghosts[0, side]
        spare = pltpu.roll(got, width + OTHER - SPARE, 1)
        ghosts[0, side] = jnp.where(here, jnp.where(begin == edge, spare, tile), got)

    def first_section(i, carry):
        @pl.when(i == layers)
        def _():
            local[0][5].wait_recv()

        a, rate = rate_of(cells0, 0, i)
        u = [cells0[c, a, body, :] + TIME_STEP * rate[c] for c in range(5)]
        turned = jnp.where(i == layers, -sigma, 0.0) * wheel
        pack(1, i, keep(cells1, i, other_frame(u, turned)))
        keep_rows(cells1, 1, i)
        return carry

    lax.fori_loop(0, layers + 1, first_section, 0)
    send(local[1])

    def second_section(i, carry):
        _, rate = rate_of(cells1, 1, i)
        for c in range(5):
            rate_ref[0, c, i] = rate[c]
            new_ref[0, c, i] = 0.5 * cells0[c, i, body, :] + 0.5 * (
                cells1[c, i, body, :] + TIME_STEP * rate[c]
            )
        return carry

    lax.fori_loop(0, layers, second_section, 0)
    for copy in local[0] + local[1]:
        copy.wait_send()


def far(shift, state, inv_volume):
    height, width = state.shape[3:]
    anywhere = pl.BlockSpec(memory_space=pl.ANY)
    return pl.pallas_call(
        functools.partial(far_kernel, shift, lax.axis_size("circ")),
        out_shape=jax.ShapeDtypeStruct((11, height, width), jnp.float32),
        in_specs=[anywhere, anywhere],
        out_specs=anywhere,
        scratch_shapes=[pltpu.SemaphoreType.DMA((3,)), pltpu.SemaphoreType.DMA((3,))],
        compiler_params=pltpu.CompilerParams(collective_id=shift + 1, has_side_effects=True),
    )(state, inv_volume)


def on_device(state, inv_volume, wheel_speed, offset):
    sectors = lax.axis_size("circ")
    layers, height, width = state.shape[2:]
    arrived = lax.switch(
        lax.rem((offset[0] + width // 2) // width, sectors),
        [functools.partial(far, shift) for shift in range(sectors)],
        state,
        inv_volume,
    )
    f32 = jnp.float32
    cells = pltpu.VMEM((QUANTITIES, layers + 4, height + 2 * PAD, width), f32)
    vmem = pl.BlockSpec(memory_space=pltpu.VMEM)
    out = jax.ShapeDtypeStruct(state.shape, f32)
    return pl.pallas_call(
        functools.partial(kernel, sectors),
        out_shape=(out, out),
        in_specs=[pl.BlockSpec(memory_space=pltpu.SMEM)] + [vmem] * 4,
        out_specs=(vmem, vmem),
        scratch_shapes=[
            cells,
            cells,
            pltpu.VMEM((layers + 1, height, width), f32),
            pltpu.VMEM((2, 2, height, width), f32),
            pltpu.VMEM((2, 2, height, width), f32),
            pltpu.VMEM((2, 8, SLOTS, width), f32),
            pltpu.VMEM((2, 8, SLOTS, width), f32),
            pltpu.VMEM((2, 11, height // 2, width), f32),
            pltpu.VMEM((2, 11, height // 2, width), f32),
            pltpu.SemaphoreType.DMA((2, 6)),
            pltpu.SemaphoreType.DMA((2, 6)),
        ],
        compiler_params=pltpu.CompilerParams(
            collective_id=0, has_side_effects=True, vmem_limit_bytes=32 * 2**20
        ),
    )(offset, wheel_speed[None, :], state, inv_volume, arrived)


def solution(mesh):
    return jax.shard_map(
        on_device,
        mesh=mesh,
        in_specs=(
            P("row", None, None, "rad", "circ"),
            P("row", None, "rad", "circ"),
            P("rad"),
            P(),
        ),
        out_specs=(P("row", None, None, "rad", "circ"), P("row", None, None, "rad", "circ")),
        check_vma=False,
    )
```

```python
import functools

import jax
import jax.numpy as jnp
from jax import lax
from jax.experimental import pallas as pl
from jax.experimental.pallas import tpu as pltpu
from jax.sharding import PartitionSpec as P

GAMMA = 1.4
TIME_STEP = 0.05
MESH = pl.DeviceIdType.MESH

V1, V2, V3, PRESSURE, SOUND = 5, 6, 7, 8, 9
QUANTITIES = 10
AXIAL = (0, 1, 2, 3, 4, V1, PRESSURE, SOUND)
RADIAL = (0, 1, 2, 3, 4, V2, PRESSURE, SOUND)
CIRCUM = (0, 1, 2, 3, 4, V3, PRESSURE, SOUND)
PAD = 8
GROUP = 8
GHOST, OTHER, BEYOND, FACING = 8, 9, 10, 11
SPARE = 12
SLOTS = 16


def quantities(u):
    inverse = 1.0 / u[0]
    v1, v2, v3 = u[1] * inverse, u[2] * inverse, u[3] * inverse
    pressure = (GAMMA - 1.0) * (u[4] - 0.5 * (u[1] * v1 + u[2] * v2 + u[3] * v3))
    return list(u) + [v1, v2, v3, pressure, jnp.sqrt(GAMMA * pressure * inverse)]


def flux(cell, component):
    speed, pressure = cell[5], cell[6]
    out = [cell[c] * speed for c in range(4)] + [(cell[4] + pressure) * speed]
    out[component] = out[component] + pressure
    return out


def add_side(total, here, there, component, sign):
    wave = jnp.maximum(jnp.abs(here[5]) + here[7], jnp.abs(there[5]) + there[7])
    moved = flux(there, component)
    for c in range(5):
        term = wave * (there[c] - here[c])
        term = term - moved[c] if sign > 0 else term + moved[c]
        total[c] = term if total[c] is None else total[c] + term


def far_kernel(shift, sectors, state_ref, volume_ref, got_ref, send_sem, recv_sem):
    row = lax.axis_index("row")
    sector = lax.axis_index("circ")
    layers = state_ref.shape[2]
    targets = []
    for way in (shift, shift + GROUP):
        near = lax.rem(sector + jnp.where(row == 0, way, sectors - way), sectors)
        targets.append({"row": 1 - row, "circ": near})
    barrier = pltpu.get_barrier_semaphore()
    for target in targets:
        pl.semaphore_signal(barrier, inc=1, device_id=target, device_id_type=MESH)
    pl.semaphore_wait(barrier, 2)
    outer = jnp.where(row == 0, layers - 1, 0)
    inner = jnp.where(row == 0, layers - 2, 1)
    copies = []
    for j, (src, at) in enumerate(
        (
            (state_ref.at[0, :, outer], pl.ds(0, 5)),
            (state_ref.at[0, :, inner], pl.ds(5, 5)),
            (volume_ref.at[:, outer], pl.ds(10, 1)),
        )
    ):
        for i, target in enumerate(targets):
            copies.append(
                pltpu.make_async_remote_copy(
                    src_ref=src,
                    dst_ref=got_ref.at[i, at],
                    send_sem=send_sem.at[j, i],
                    recv_sem=recv_sem.at[j, i],
                    device_id=target,
                    device_id_type=MESH,
                )
            )
    for copy in copies:
        copy.start()
    for copy in copies:
        copy.wait()


def kernel(
    sectors,
    offset_ref,
    wheel_ref,
    state_ref,
    volume_ref,
    far_ref,
    new_ref,
    rate_ref,
    cells0,
    cells1,
    volumes,
    packed,
    ghosts,
    edges,
    rows,
    halves_out,
    halves_in,
    send_sem,
    recv_sem,
):
    row = lax.axis_index("row")
    sector = lax.axis_index("circ")
    rad = lax.axis_index("rad")
    layers, height, width = state_ref.shape[2:]
    left = {"circ": lax.rem(sector + sectors - 1, sectors)}
    right = {"circ": lax.rem(sector + 1, sectors)}
    beside = {"rad": 1 - rad}
    barrier = pltpu.get_barrier_semaphore()
    for device in (left, right, beside):
        pl.semaphore_signal(barrier, inc=1, device_id=device, device_id_type=MESH)

    sigma = (1 - 2 * row).astype(jnp.float32)
    face_layer = jnp.where(row == 0, layers - 1, 0)
    lanes = lax.broadcasted_iota(jnp.int32, (height, width), 1)
    inner_row = PAD + jnp.where(rad == 0, height - 1, 0)
    inner_pad = PAD + jnp.where(rad == 0, height, -1)
    wall_row = PAD + jnp.where(rad == 0, 0, height - 1)
    wall_pad = PAD + jnp.where(rad == 0, -1, height)
    diagonal = lax.broadcasted_iota(jnp.int32, (height, height), 0) == lax.broadcasted_iota(
        jnp.int32, (height, height), 1
    )
    wheel = jnp.sum(
        jnp.where(diagonal, jnp.broadcast_to(wheel_ref[...], (height, height)), 0.0),
        axis=1,
        keepdims=True,
    )
    rest = lax.rem(offset_ref[0] + width // 2, width)
    pick = lax.rem((offset_ref[0] + width // 2) // (width * GROUP), 2)
    turn = jnp.where(row == 0, lax.rem(width - rest, width), rest)
    low_lanes = lanes < jnp.where(row == 0, width - rest, rest)
    body = pl.ds(PAD, height)

    def other_frame(u, speed):
        return [
            u[0],
            u[1],
            u[2],
            u[3] + u[0] * speed,
            u[4] + u[3] * speed + 0.5 * u[0] * speed * speed,
        ]

    half_width, half_height = width // 2, height // 2
    low_half = lanes < half_width
    low_top = lanes[:half_height] < half_width

    def split(c):
        top, bottom = far_ref[pick, c, :half_height], far_ref[pick, c, half_height:]
        halves_out[0, c] = jnp.where(low_top, top, pltpu.roll(bottom, half_width, 1))
        halves_out[1, c] = jnp.where(low_top, pltpu.roll(top, half_width, 1), bottom)

    def turned(c):
        middle = pltpu.roll(far_ref[pick, c], half_width, 1)
        late, early = halves_in[0, c], halves_in[1, c]
        before = jnp.concatenate([early, pltpu.roll(early, half_width, 1)])
        after = jnp.concatenate([pltpu.roll(late, half_width, 1), late])
        return (
            pltpu.roll(jnp.where(low_half, before, middle), turn, 1),
            pltpu.roll(jnp.where(low_half, middle, after), turn, 1),
        )

    def window(c):
        low, high = turned(c)
        return jnp.where(low_lanes, low, high)

    def keep(cells, a, u):
        values = quantities(u)
        for q in range(QUANTITIES):
            cells[q, a, body, :] = values[q]
        return values

    def columns(a, firsts, lasts):
        first = jnp.zeros((height, width), jnp.float32)
        last = first
        for i, q in enumerate(CIRCUM):
            here = lanes == SLOTS * i
            x = firsts[q]
            first = jnp.where(here, pltpu.roll(x, SLOTS * i, 1) if i else x, first)
            last = jnp.where(here, pltpu.roll(lasts[q], SLOTS * i + 1, 1), last)
        return pltpu.roll(first, a, 1), pltpu.roll(last, a, 1)

    def pack(round_, a, values):
        here = lax.rem(lanes, SLOTS) == a
        for side, tile in enumerate(columns(a, values, values)):
            packed[round_, side] = jnp.where(here, tile, packed[round_, side])

    def keep_rows(cells, round_, a):
        for i, q in enumerate(RADIAL):
            rows[round_, i, pl.ds(a, 1), :] = cells[q, a, pl.ds(inner_row, 1), :]
            wall = cells[q, a, pl.ds(wall_row, 1), :]
            cells[q, a, pl.ds(wall_pad, 1), :] = -wall if q in (2, V2) else wall

    def rate_of(cells, round_, i):
        a = jnp.where(i == layers, OTHER, i)
        below = jnp.where(row == 0, jnp.maximum(i - 1, 0), jnp.where(i == 0, GHOST, i - 1))
        below = jnp.where(i == layers, jnp.where(row == 0, FACING, BEYOND), below)
        above = jnp.where(row == 0, i + 1, jnp.minimum(i + 1, layers - 1))
        above = jnp.where(i == layers, jnp.where(row == 0, BEYOND, FACING), above)
        for j, q in enumerate(RADIAL):
            cells[q, a, pl.ds(inner_pad, 1), :] = edges[round_, j, pl.ds(a, 1), :]

        def layer(qs, slot, by=0):
            return [cells[q, slot, pl.ds(PAD + by, height), :] for q in qs]

        total = [None] * 5
        here = layer(AXIAL, a)
        add_side(total, here, layer(AXIAL, above), 1, 1)
        add_side(total, here, layer(AXIAL, below), 1, -1)
        here = layer(RADIAL, a)
        add_side(total, here, layer(RADIAL, a, 1), 2, 1)
        add_side(total, here, layer(RADIAL, a, -1), 2, -1)
        here = layer(CIRCUM, a)
        before = pltpu.roll(ghosts[round_, 0], lax.rem(width - a, width), 1)
        after = pltpu.roll(ghosts[round_, 1], width - 1 - a, 1)
        up, down = [], []
        for j in range(8):
            ghost = pltpu.roll(after, width - SLOTS * j, 1) if j else after
            up.append(jnp.where(lanes == width - 1, ghost, pltpu.roll(here[j], width - 1, 1)))
            ghost = pltpu.roll(before, width - SLOTS * j, 1) if j else before
            down.append(jnp.where(lanes == 0, ghost, pltpu.roll(here[j], 1, 1)))
        add_side(total, here, up, 3, 1)
        add_side(total, here, down, 3, -1)
        half = 0.5 * volumes[i]
        return a, [half * part for part in total]

    def local_copies(round_):
        return [
            pltpu.make_async_remote_copy(
                src_ref=src,
                dst_ref=dst,
                send_sem=send_sem.at[round_, i],
                recv_sem=recv_sem.at[round_, i],
                device_id=device,
                device_id_type=MESH,
            )
            for i, (src, dst, device) in enumerate(
                (
                    (packed.at[round_, 0], ghosts.at[round_, 1], left),
                    (packed.at[round_, 1], ghosts.at[round_, 0], right),
                    (rows.at[round_, :, pl.ds(0, 8)], edges.at[round_, :, pl.ds(0, 8)], beside),
                    (halves_out.at[0], halves_in.at[0], left),
                    (halves_out.at[1], halves_in.at[1], right),
                    (rows.at[round_, :, pl.ds(8, 8)], edges.at[round_, :, pl.ds(8, 8)], beside),
                )
            )
            if round_ == 0 or i < 3
        ]

    def send(copies):
        for copy in copies:
            copy.start()
        for copy in copies:
            copy.wait_recv()

    local = [local_copies(r) for r in range(2)]
    for r in range(2):
        packed[r] = jnp.zeros_like(packed[r])
        rows[r] = jnp.zeros_like(rows[r])

    def prepare(a, carry):
        pack(0, a, keep(cells0, a, [state_ref[0, c, a] for c in range(5)]))
        keep_rows(cells0, 0, a)
        volumes[a] = volume_ref[0, a]
        return carry

    lax.fori_loop(0, layers, prepare, 0)
    for c in range(11):
        split(c)
    middle = [pltpu.roll(far_ref[pick, c], half_width, 1) for c in range(5)]
    pack(0, SPARE, quantities(middle))

    pl.semaphore_wait(barrier, 3)
    for copy in local[0][:5]:
        copy.start()
    mine = [state_ref[0, c, face_layer] for c in range(5)]
    keep(cells0, FACING, other_frame(mine, sigma * wheel))
    for copy in local[0][:5]:
        copy.wait_recv()

    pairs = [turned(c) for c in range(5)]
    other = [jnp.where(low_lanes, low, high) for low, high in pairs]
    keep(cells0, OTHER, other)
    keep_rows(cells0, 0, OTHER)
    local[0][5].start()
    keep(cells0, GHOST, other_frame(other, -sigma * wheel))
    keep(cells0, BEYOND, [window(5 + c) for c in range(5)])
    volumes[layers] = window(10)
    late, early = columns(
        OTHER, quantities([high for _, high in pairs]), quantities([low for low, _ in pairs])
    )
    begin = jnp.where(row == 0, rest, width - rest)
    here = lax.rem(lanes, SLOTS) == OTHER
    for side, tile, edge in ((0, early, 0), (1, late, width)):
        got = ghosts[0, side]
        spare = pltpu.roll(got, width + OTHER - SPARE, 1)
        ghosts[0, side] = jnp.where(here, jnp.where(begin == edge, spare, tile), got)

    def first_section(i, carry):
        @pl.when(i == layers)
        def _():
            local[0][5].wait_recv()

        a, rate = rate_of(cells0, 0, i)
        u = [cells0[c, a, body, :] + TIME_STEP * rate[c] for c in range(5)]
        turned = jnp.where(i == layers, -sigma, 0.0) * wheel
        pack(1, i, keep(cells1, i, other_frame(u, turned)))
        keep_rows(cells1, 1, i)
        return carry

    lax.fori_loop(0, layers + 1, first_section, 0)
    send(local[1])

    def second_section(i, carry):
        _, rate = rate_of(cells1, 1, i)
        for c in range(5):
            rate_ref[0, c, i] = rate[c]
            new_ref[0, c, i] = 0.5 * cells0[c, i, body, :] + 0.5 * (
                cells1[c, i, body, :] + TIME_STEP * rate[c]
            )
        return carry

    lax.fori_loop(0, layers, second_section, 0)
    for copy in local[0] + local[1]:
        copy.wait_send()


def far(shift, state, inv_volume):
    height, width = state.shape[3:]
    anywhere = pl.BlockSpec(memory_space=pl.ANY)
    return pl.pallas_call(
        functools.partial(far_kernel, shift, lax.axis_size("circ")),
        out_shape=jax.ShapeDtypeStruct((2, 11, height, width), jnp.float32),
        in_specs=[anywhere, anywhere],
        out_specs=anywhere,
        scratch_shapes=[pltpu.SemaphoreType.DMA((3, 2)), pltpu.SemaphoreType.DMA((3, 2))],
        compiler_params=pltpu.CompilerParams(collective_id=1 + shift // 2 // GROUP * GROUP + shift % GROUP, has_side_effects=True),
    )(state, inv_volume)


def on_device(state, inv_volume, wheel_speed, offset):
    sectors = lax.axis_size("circ")
    layers, height, width = state.shape[2:]
    whole = lax.rem((offset[0] + width // 2) // width, sectors)
    arrived = lax.switch(
        whole // (2 * GROUP) * GROUP + lax.rem(whole, GROUP),
        [
            functools.partial(far, first + shift)
            for first in range(0, sectors, 2 * GROUP)
            for shift in range(GROUP)
        ],
        state,
        inv_volume,
    )
    f32 = jnp.float32
    cells = pltpu.VMEM((QUANTITIES, layers + 4, height + 2 * PAD, width), f32)
    vmem = pl.BlockSpec(memory_space=pltpu.VMEM)
    out = jax.ShapeDtypeStruct(state.shape, f32)
    return pl.pallas_call(
        functools.partial(kernel, sectors),
        out_shape=(out, out),
        in_specs=[pl.BlockSpec(memory_space=pltpu.SMEM)] + [vmem] * 4,
        out_specs=(vmem, vmem),
        scratch_shapes=[
            cells,
            cells,
            pltpu.VMEM((layers + 1, height, width), f32),
            pltpu.VMEM((2, 2, height, width), f32),
            pltpu.VMEM((2, 2, height, width), f32),
            pltpu.VMEM((2, 8, SLOTS, width), f32),
            pltpu.VMEM((2, 8, SLOTS, width), f32),
            pltpu.VMEM((2, 11, height // 2, width), f32),
            pltpu.VMEM((2, 11, height // 2, width), f32),
            pltpu.SemaphoreType.DMA((2, 6)),
            pltpu.SemaphoreType.DMA((2, 6)),
        ],
        compiler_params=pltpu.CompilerParams(
            collective_id=0, has_side_effects=True, vmem_limit_bytes=32 * 2**20
        ),
    )(offset, wheel_speed[None, :], state, inv_volume, arrived)


def solution(mesh):
    return jax.shard_map(
        on_device,
        mesh=mesh,
        in_specs=(
            P("row", None, None, "rad", "circ"),
            P("row", None, "rad", "circ"),
            P("rad"),
            P(),
        ),
        out_specs=(P("row", None, None, "rad", "circ"), P("row", None, None, "rad", "circ")),
        check_vma=False,
    )
```

```python
import functools

import jax
import jax.numpy as jnp
from jax import lax
from jax.experimental import pallas as pl
from jax.experimental.pallas import tpu as pltpu
from jax.sharding import PartitionSpec as P

GAMMA = 1.4
TIME_STEP = 0.05
MESH = pl.DeviceIdType.MESH

V1, V2, V3, PRESSURE, SOUND = 5, 6, 7, 8, 9
QUANTITIES = 10
AXIAL = (0, 1, 2, 3, 4, V1, PRESSURE, SOUND)
RADIAL = (0, 1, 2, 3, 4, V2, PRESSURE, SOUND)
CIRCUM = (0, 1, 2, 3, 4, V3, PRESSURE, SOUND)
PAD = 8
GROUP = 8
GHOST, OTHER, BEYOND, FACING = 8, 9, 10, 11
SPARE = 12
SLOTS = 16


def quantities(u):
    inverse = 1.0 / u[0]
    v1, v2, v3 = u[1] * inverse, u[2] * inverse, u[3] * inverse
    pressure = (GAMMA - 1.0) * (u[4] - 0.5 * (u[1] * v1 + u[2] * v2 + u[3] * v3))
    return list(u) + [v1, v2, v3, pressure, jnp.sqrt(GAMMA * pressure * inverse)]


def flux(cell, component):
    speed, pressure = cell[5], cell[6]
    out = [cell[c] * speed for c in range(4)] + [(cell[4] + pressure) * speed]
    out[component] = out[component] + pressure
    return out


def add_side(total, here, there, component, sign):
    wave = jnp.maximum(jnp.abs(here[5]) + here[7], jnp.abs(there[5]) + there[7])
    moved = flux(there, component)
    for c in range(5):
        term = wave * (there[c] - here[c])
        term = term - moved[c] if sign > 0 else term + moved[c]
        total[c] = term if total[c] is None else total[c] + term


def far_kernel(shift, sectors, state_ref, volume_ref, got_ref, send_sem, recv_sem):
    row = lax.axis_index("row")
    sector = lax.axis_index("circ")
    layers = state_ref.shape[2]
    targets = []
    for way in (shift, shift + GROUP):
        near = lax.rem(sector + jnp.where(row == 0, way, sectors - way), sectors)
        targets.append({"row": 1 - row, "circ": near})
    barrier = pltpu.get_barrier_semaphore()
    for target in targets:
        pl.semaphore_signal(barrier, inc=1, device_id=target, device_id_type=MESH)
    pl.semaphore_wait(barrier, 2)
    outer = jnp.where(row == 0, layers - 1, 0)
    inner = jnp.where(row == 0, layers - 2, 1)
    copies = []
    for j, (src, at) in enumerate(
        (
            (state_ref.at[0, :, outer], pl.ds(0, 5)),
            (state_ref.at[0, :, inner], pl.ds(5, 5)),
            (volume_ref.at[:, outer], pl.ds(10, 1)),
        )
    ):
        for i, target in enumerate(targets):
            copies.append(
                pltpu.make_async_remote_copy(
                    src_ref=src,
                    dst_ref=got_ref.at[i, at],
                    send_sem=send_sem.at[j, i],
                    recv_sem=recv_sem.at[j, i],
                    device_id=target,
                    device_id_type=MESH,
                )
            )
    for copy in copies:
        copy.start()
    for copy in copies:
        copy.wait()


def kernel(
    sectors,
    offset_ref,
    wheel_ref,
    state_ref,
    volume_ref,
    far_ref,
    new_ref,
    rate_ref,
    cells0,
    cells1,
    volumes,
    sums,
    packed,
    ghosts,
    edges,
    rows,
    halves_out,
    halves_in,
    send_sem,
    recv_sem,
):
    row = lax.axis_index("row")
    sector = lax.axis_index("circ")
    rad = lax.axis_index("rad")
    layers, height, width = state_ref.shape[2:]
    left = {"circ": lax.rem(sector + sectors - 1, sectors)}
    right = {"circ": lax.rem(sector + 1, sectors)}
    beside = {"rad": 1 - rad}
    barrier = pltpu.get_barrier_semaphore()
    for device in (left, right, beside):
        pl.semaphore_signal(barrier, inc=1, device_id=device, device_id_type=MESH)

    sigma = (1 - 2 * row).astype(jnp.float32)
    face_layer = jnp.where(row == 0, layers - 1, 0)
    lanes = lax.broadcasted_iota(jnp.int32, (height, width), 1)
    inner_row = PAD + jnp.where(rad == 0, height - 1, 0)
    inner_pad = PAD + jnp.where(rad == 0, height, -1)
    wall_row = PAD + jnp.where(rad == 0, 0, height - 1)
    wall_pad = PAD + jnp.where(rad == 0, -1, height)
    diagonal = lax.broadcasted_iota(jnp.int32, (height, height), 0) == lax.broadcasted_iota(
        jnp.int32, (height, height), 1
    )
    wheel = jnp.sum(
        jnp.where(diagonal, jnp.broadcast_to(wheel_ref[...], (height, height)), 0.0),
        axis=1,
        keepdims=True,
    )
    rest = lax.rem(offset_ref[0] + width // 2, width)
    pick = lax.rem((offset_ref[0] + width // 2) // (width * GROUP), 2)
    turn = jnp.where(row == 0, lax.rem(width - rest, width), rest)
    low_lanes = lanes < jnp.where(row == 0, width - rest, rest)
    body = pl.ds(PAD, height)

    def other_frame(u, speed):
        return [
            u[0],
            u[1],
            u[2],
            u[3] + u[0] * speed,
            u[4] + u[3] * speed + 0.5 * u[0] * speed * speed,
        ]

    half_width, half_height = width // 2, height // 2
    low_half = lanes < half_width
    low_top = lanes[:half_height] < half_width

    def split(c):
        top, bottom = far_ref[pick, c, :half_height], far_ref[pick, c, half_height:]
        halves_out[0, c] = jnp.where(low_top, top, pltpu.roll(bottom, half_width, 1))
        halves_out[1, c] = jnp.where(low_top, pltpu.roll(top, half_width, 1), bottom)

    def turned(c):
        middle = pltpu.roll(far_ref[pick, c], half_width, 1)
        late, early = halves_in[0, c], halves_in[1, c]
        before = jnp.concatenate([early, pltpu.roll(early, half_width, 1)])
        after = jnp.concatenate([pltpu.roll(late, half_width, 1), late])
        return (
            pltpu.roll(jnp.where(low_half, before, middle), turn, 1),
            pltpu.roll(jnp.where(low_half, middle, after), turn, 1),
        )

    def window(c):
        low, high = turned(c)
        return jnp.where(low_lanes, low, high)

    def keep(cells, a, u):
        values = quantities(u)
        for q in range(QUANTITIES):
            cells[q, a, body, :] = values[q]
        return values

    def columns(a, firsts, lasts):
        first = jnp.zeros((height, width), jnp.float32)
        last = first
        for i, q in enumerate(CIRCUM):
            here = lanes == SLOTS * i
            x = firsts[q]
            first = jnp.where(here, pltpu.roll(x, SLOTS * i, 1) if i else x, first)
            last = jnp.where(here, pltpu.roll(lasts[q], SLOTS * i + 1, 1), last)
        return pltpu.roll(first, a, 1), pltpu.roll(last, a, 1)

    def pack(round_, a, values):
        here = lax.rem(lanes, SLOTS) == a
        for side, tile in enumerate(columns(a, values, values)):
            packed[round_, side] = jnp.where(here, tile, packed[round_, side])

    def keep_rows(cells, round_, a):
        for i, q in enumerate(RADIAL):
            rows[round_, i, pl.ds(a, 1), :] = cells[q, a, pl.ds(inner_row, 1), :]
            wall = cells[q, a, pl.ds(wall_row, 1), :]
            cells[q, a, pl.ds(wall_pad, 1), :] = -wall if q in (2, V2) else wall

    def without_circ(cells, round_, i):
        a = jnp.where(i == layers, OTHER, i)
        below = jnp.where(row == 0, jnp.maximum(i - 1, 0), jnp.where(i == 0, GHOST, i - 1))
        below = jnp.where(i == layers, jnp.where(row == 0, FACING, BEYOND), below)
        above = jnp.where(row == 0, i + 1, jnp.minimum(i + 1, layers - 1))
        above = jnp.where(i == layers, jnp.where(row == 0, BEYOND, FACING), above)
        for j, q in enumerate(RADIAL):
            cells[q, a, pl.ds(inner_pad, 1), :] = edges[round_, j, pl.ds(a, 1), :]

        def layer(qs, slot, by=0):
            return [cells[q, slot, pl.ds(PAD + by, height), :] for q in qs]

        total = [None] * 5
        here = layer(AXIAL, a)
        add_side(total, here, layer(AXIAL, above), 1, 1)
        add_side(total, here, layer(AXIAL, below), 1, -1)
        here = layer(RADIAL, a)
        add_side(total, here, layer(RADIAL, a, 1), 2, 1)
        add_side(total, here, layer(RADIAL, a, -1), 2, -1)
        for c in range(5):
            sums[c, i] = total[c]

    def rate_of(cells, round_, i):
        a = jnp.where(i == layers, OTHER, i)
        total = [sums[c, i] for c in range(5)]
        here = [cells[q, a, body, :] for q in CIRCUM]
        before = pltpu.roll(ghosts[round_, 0], lax.rem(width - a, width), 1)
        after = pltpu.roll(ghosts[round_, 1], width - 1 - a, 1)
        up, down = [], []
        for j in range(8):
            ghost = pltpu.roll(after, width - SLOTS * j, 1) if j else after
            up.append(jnp.where(lanes == width - 1, ghost, pltpu.roll(here[j], width - 1, 1)))
            ghost = pltpu.roll(before, width - SLOTS * j, 1) if j else before
            down.append(jnp.where(lanes == 0, ghost, pltpu.roll(here[j], 1, 1)))
        add_side(total, here, up, 3, 1)
        add_side(total, here, down, 3, -1)
        half = 0.5 * volumes[i]
        return a, [half * part for part in total]

    def local_copies(round_):
        return [
            pltpu.make_async_remote_copy(
                src_ref=src,
                dst_ref=dst,
                send_sem=send_sem.at[round_, i],
                recv_sem=recv_sem.at[round_, i],
                device_id=device,
                device_id_type=MESH,
            )
            for i, (src, dst, device) in enumerate(
                (
                    (packed.at[round_, 0], ghosts.at[round_, 1], left),
                    (packed.at[round_, 1], ghosts.at[round_, 0], right),
                    (rows.at[round_, :, pl.ds(0, 8)], edges.at[round_, :, pl.ds(0, 8)], beside),
                    (halves_out.at[0], halves_in.at[0], left),
                    (halves_out.at[1], halves_in.at[1], right),
                    (rows.at[round_, :, pl.ds(8, 8)], edges.at[round_, :, pl.ds(8, 8)], beside),
                )
            )
            if round_ == 0 or i < 3
        ]

    local = [local_copies(r) for r in range(2)]
    for r in range(2):
        packed[r] = jnp.zeros_like(packed[r])
        rows[r] = jnp.zeros_like(rows[r])

    def prepare(a, carry):
        pack(0, a, keep(cells0, a, [state_ref[0, c, a] for c in range(5)]))
        keep_rows(cells0, 0, a)
        volumes[a] = volume_ref[0, a]
        return carry

    lax.fori_loop(0, layers, prepare, 0)
    for c in range(11):
        split(c)
    middle = [pltpu.roll(far_ref[pick, c], half_width, 1) for c in range(5)]
    pack(0, SPARE, quantities(middle))

    pl.semaphore_wait(barrier, 3)
    for copy in local[0][:5]:
        copy.start()
    mine = [state_ref[0, c, face_layer] for c in range(5)]
    keep(cells0, FACING, other_frame(mine, sigma * wheel))
    local[0][2].wait_recv()

    def early_layers(j, carry):
        without_circ(cells0, 0, j + row)
        return carry

    lax.fori_loop(0, layers - 1, early_layers, 0)
    for i in (0, 1, 3, 4):
        local[0][i].wait_recv()

    pairs = [turned(c) for c in range(5)]
    other = [jnp.where(low_lanes, low, high) for low, high in pairs]
    keep(cells0, OTHER, other)
    keep_rows(cells0, 0, OTHER)
    local[0][5].start()
    keep(cells0, GHOST, other_frame(other, -sigma * wheel))
    keep(cells0, BEYOND, [window(5 + c) for c in range(5)])
    volumes[layers] = window(10)
    late, early = columns(
        OTHER, quantities([high for _, high in pairs]), quantities([low for low, _ in pairs])
    )
    begin = jnp.where(row == 0, rest, width - rest)
    here = lax.rem(lanes, SLOTS) == OTHER
    for side, tile, edge in ((0, early, 0), (1, late, width)):
        got = ghosts[0, side]
        spare = pltpu.roll(got, width + OTHER - SPARE, 1)
        ghosts[0, side] = jnp.where(here, jnp.where(begin == edge, spare, tile), got)

    without_circ(cells0, 0, face_layer)

    def first_section(i, carry):
        @pl.when(i == layers)
        def _():
            local[0][5].wait_recv()
            without_circ(cells0, 0, layers)

        a, rate = rate_of(cells0, 0, i)
        u = [cells0[c, a, body, :] + TIME_STEP * rate[c] for c in range(5)]
        turned = jnp.where(i == layers, -sigma, 0.0) * wheel
        pack(1, i, keep(cells1, i, other_frame(u, turned)))
        keep_rows(cells1, 1, i)
        return carry

    lax.fori_loop(0, layers + 1, first_section, 0)
    for copy in local[1]:
        copy.start()
    local[1][2].wait_recv()

    def second_early(i, carry):
        without_circ(cells1, 1, i)
        return carry

    lax.fori_loop(0, layers, second_early, 0)
    local[1][0].wait_recv()
    local[1][1].wait_recv()

    def second_section(i, carry):
        _, rate = rate_of(cells1, 1, i)
        for c in range(5):
            rate_ref[0, c, i] = rate[c]
            new_ref[0, c, i] = 0.5 * cells0[c, i, body, :] + 0.5 * (
                cells1[c, i, body, :] + TIME_STEP * rate[c]
            )
        return carry

    lax.fori_loop(0, layers, second_section, 0)
    for copy in local[0] + local[1]:
        copy.wait_send()


def far(shift, state, inv_volume):
    height, width = state.shape[3:]
    anywhere = pl.BlockSpec(memory_space=pl.ANY)
    return pl.pallas_call(
        functools.partial(far_kernel, shift, lax.axis_size("circ")),
        out_shape=jax.ShapeDtypeStruct((2, 11, height, width), jnp.float32),
        in_specs=[anywhere, anywhere],
        out_specs=anywhere,
        scratch_shapes=[pltpu.SemaphoreType.DMA((3, 2)), pltpu.SemaphoreType.DMA((3, 2))],
        compiler_params=pltpu.CompilerParams(collective_id=1 + shift // 2 // GROUP * GROUP + shift % GROUP, has_side_effects=True),
    )(state, inv_volume)


def on_device(state, inv_volume, wheel_speed, offset):
    sectors = lax.axis_size("circ")
    layers, height, width = state.shape[2:]
    whole = lax.rem((offset[0] + width // 2) // width, sectors)
    arrived = lax.switch(
        whole // (2 * GROUP) * GROUP + lax.rem(whole, GROUP),
        [
            functools.partial(far, first + shift)
            for first in range(0, sectors, 2 * GROUP)
            for shift in range(GROUP)
        ],
        state,
        inv_volume,
    )
    f32 = jnp.float32
    cells = pltpu.VMEM((QUANTITIES, layers + 4, height + 2 * PAD, width), f32)
    vmem = pl.BlockSpec(memory_space=pltpu.VMEM)
    out = jax.ShapeDtypeStruct(state.shape, f32)
    return pl.pallas_call(
        functools.partial(kernel, sectors),
        out_shape=(out, out),
        in_specs=[pl.BlockSpec(memory_space=pltpu.SMEM)] + [vmem] * 4,
        out_specs=(vmem, vmem),
        scratch_shapes=[
            cells,
            cells,
            pltpu.VMEM((layers + 1, height, width), f32),
            pltpu.VMEM((5, layers + 1, height, width), f32),
            pltpu.VMEM((2, 2, height, width), f32),
            pltpu.VMEM((2, 2, height, width), f32),
            pltpu.VMEM((2, 8, SLOTS, width), f32),
            pltpu.VMEM((2, 8, SLOTS, width), f32),
            pltpu.VMEM((2, 11, height // 2, width), f32),
            pltpu.VMEM((2, 11, height // 2, width), f32),
            pltpu.SemaphoreType.DMA((2, 6)),
            pltpu.SemaphoreType.DMA((2, 6)),
        ],
        compiler_params=pltpu.CompilerParams(
            collective_id=0, has_side_effects=True, vmem_limit_bytes=32 * 2**20
        ),
    )(offset, wheel_speed[None, :], state, inv_volume, arrived)


def solution(mesh):
    return jax.shard_map(
        on_device,
        mesh=mesh,
        in_specs=(
            P("row", None, None, "rad", "circ"),
            P("row", None, "rad", "circ"),
            P("rad"),
            P(),
        ),
        out_specs=(P("row", None, None, "rad", "circ"), P("row", None, None, "rad", "circ")),
        check_vma=False,
    )
```

```python
import functools

import jax
import jax.numpy as jnp
from jax import lax
from jax.experimental import pallas as pl
from jax.experimental.pallas import tpu as pltpu
from jax.sharding import PartitionSpec as P

GAMMA = 1.4
TIME_STEP = 0.05
MESH = pl.DeviceIdType.MESH

V1, V2, V3, PRESSURE, SOUND = 5, 6, 7, 8, 9
QUANTITIES = 10
AXIAL = (0, 1, 2, 3, 4, V1, PRESSURE, SOUND)
RADIAL = (0, 1, 2, 3, 4, V2, PRESSURE, SOUND)
CIRCUM = (0, 1, 2, 3, 4, V3, PRESSURE, SOUND)
PAD = 8
GROUP = 8
GHOST, OTHER, BEYOND, FACING = 8, 9, 10, 11
SPARE = 12
SLOTS = 16


def quantities(u):
    inverse = 1.0 / u[0]
    v1, v2, v3 = u[1] * inverse, u[2] * inverse, u[3] * inverse
    pressure = (GAMMA - 1.0) * (u[4] - 0.5 * (u[1] * v1 + u[2] * v2 + u[3] * v3))
    return list(u) + [v1, v2, v3, pressure, jnp.sqrt(GAMMA * pressure * inverse)]


def flux(cell, component):
    speed, pressure = cell[5], cell[6]
    out = [cell[c] * speed for c in range(4)] + [(cell[4] + pressure) * speed]
    out[component] = out[component] + pressure
    return out


def add_side(total, here, there, component, sign):
    wave = jnp.maximum(jnp.abs(here[5]) + here[7], jnp.abs(there[5]) + there[7])
    moved = flux(there, component)
    for c in range(5):
        term = wave * (there[c] - here[c])
        term = term - moved[c] if sign > 0 else term + moved[c]
        total[c] = term if total[c] is None else total[c] + term


def far_kernel(shift, sectors, state_ref, volume_ref, got_ref, send_sem, recv_sem):
    row = lax.axis_index("row")
    sector = lax.axis_index("circ")
    layers = state_ref.shape[2]
    targets = []
    for way in (shift, shift + GROUP):
        near = lax.rem(sector + jnp.where(row == 0, way, sectors - way), sectors)
        targets.append({"row": 1 - row, "circ": near})
    barrier = pltpu.get_barrier_semaphore()
    for target in targets:
        pl.semaphore_signal(barrier, inc=1, device_id=target, device_id_type=MESH)
    pl.semaphore_wait(barrier, 2)
    outer = jnp.where(row == 0, layers - 1, 0)
    inner = jnp.where(row == 0, layers - 2, 1)
    copies = []
    for j, (src, at) in enumerate(
        (
            (state_ref.at[0, :, outer], pl.ds(0, 5)),
            (state_ref.at[0, :, inner], pl.ds(5, 5)),
            (volume_ref.at[:, outer], pl.ds(10, 1)),
        )
    ):
        for i, target in enumerate(targets):
            copies.append(
                pltpu.make_async_remote_copy(
                    src_ref=src,
                    dst_ref=got_ref.at[i, at],
                    send_sem=send_sem.at[j, i],
                    recv_sem=recv_sem.at[j, i],
                    device_id=target,
                    device_id_type=MESH,
                )
            )
    for copy in copies:
        copy.start()
    for copy in copies:
        copy.wait()


def kernel(
    sectors,
    offset_ref,
    wheel_ref,
    state_ref,
    volume_ref,
    far_ref,
    new_ref,
    rate_ref,
    cells0,
    cells1,
    volumes,
    sums,
    packed,
    ghosts,
    edges,
    rows,
    halves_out,
    halves_in,
    send_sem,
    recv_sem,
):
    row = lax.axis_index("row")
    sector = lax.axis_index("circ")
    rad = lax.axis_index("rad")
    layers, height, width = state_ref.shape[2:]
    left = {"circ": lax.rem(sector + sectors - 1, sectors)}
    right = {"circ": lax.rem(sector + 1, sectors)}
    beside = {"rad": 1 - rad}
    barrier = pltpu.get_barrier_semaphore()
    for device in (left, right, beside):
        pl.semaphore_signal(barrier, inc=1, device_id=device, device_id_type=MESH)

    sigma = (1 - 2 * row).astype(jnp.float32)
    face_layer = jnp.where(row == 0, layers - 1, 0)
    lanes = lax.broadcasted_iota(jnp.int32, (height, width), 1)
    inner_row = PAD + jnp.where(rad == 0, height - 1, 0)
    inner_pad = PAD + jnp.where(rad == 0, height, -1)
    wall_row = PAD + jnp.where(rad == 0, 0, height - 1)
    wall_pad = PAD + jnp.where(rad == 0, -1, height)
    diagonal = lax.broadcasted_iota(jnp.int32, (height, height), 0) == lax.broadcasted_iota(
        jnp.int32, (height, height), 1
    )
    wheel = jnp.sum(
        jnp.where(diagonal, jnp.broadcast_to(wheel_ref[...], (height, height)), 0.0),
        axis=1,
        keepdims=True,
    )
    rest = lax.rem(offset_ref[0] + width // 2, width)
    pick = lax.rem((offset_ref[0] + width // 2) // (width * GROUP), 2)
    turn = jnp.where(row == 0, lax.rem(width - rest, width), rest)
    low_lanes = lanes < jnp.where(row == 0, width - rest, rest)
    body = pl.ds(PAD, height)

    def other_frame(u, speed):
        return [
            u[0],
            u[1],
            u[2],
            u[3] + u[0] * speed,
            u[4] + u[3] * speed + 0.5 * u[0] * speed * speed,
        ]

    half_width, half_height = width // 2, height // 2
    low_half = lanes < half_width
    low_top = lanes[:half_height] < half_width

    def split(c):
        top, bottom = far_ref[pick, c, :half_height], far_ref[pick, c, half_height:]
        halves_out[0, c] = jnp.where(low_top, top, pltpu.roll(bottom, half_width, 1))
        halves_out[1, c] = jnp.where(low_top, pltpu.roll(top, half_width, 1), bottom)

    def turned(c):
        middle = pltpu.roll(far_ref[pick, c], half_width, 1)
        late, early = halves_in[0, c], halves_in[1, c]
        before = jnp.concatenate([early, pltpu.roll(early, half_width, 1)])
        after = jnp.concatenate([pltpu.roll(late, half_width, 1), late])
        return (
            pltpu.roll(jnp.where(low_half, before, middle), turn, 1),
            pltpu.roll(jnp.where(low_half, middle, after), turn, 1),
        )

    def window(c):
        low, high = turned(c)
        return jnp.where(low_lanes, low, high)

    def keep(cells, a, u):
        values = quantities(u)
        for q in range(QUANTITIES):
            cells[q, a, body, :] = values[q]
        return values

    def columns(a, firsts, lasts):
        first = jnp.zeros((height, width), jnp.float32)
        last = first
        for i, q in enumerate(CIRCUM):
            here = lanes == SLOTS * i
            x = firsts[q]
            first = jnp.where(here, pltpu.roll(x, SLOTS * i, 1) if i else x, first)
            last = jnp.where(here, pltpu.roll(lasts[q], SLOTS * i + 1, 1), last)
        return pltpu.roll(first, a, 1), pltpu.roll(last, a, 1)

    def pack(round_, a, values):
        here = lax.rem(lanes, SLOTS) == a
        for side, tile in enumerate(columns(a, values, values)):
            packed[round_, side] = jnp.where(here, tile, packed[round_, side])

    def keep_rows(cells, round_, a):
        for i, q in enumerate(RADIAL):
            rows[round_, i, pl.ds(a, 1), :] = cells[q, a, pl.ds(inner_row, 1), :]
            wall = cells[q, a, pl.ds(wall_row, 1), :]
            cells[q, a, pl.ds(wall_pad, 1), :] = -wall if q in (2, V2) else wall

    def without_circ(cells, round_, i):
        a = jnp.where(i == layers, OTHER, i)
        below = jnp.where(row == 0, jnp.maximum(i - 1, 0), jnp.where(i == 0, GHOST, i - 1))
        below = jnp.where(i == layers, jnp.where(row == 0, FACING, BEYOND), below)
        above = jnp.where(row == 0, i + 1, jnp.minimum(i + 1, layers - 1))
        above = jnp.where(i == layers, jnp.where(row == 0, BEYOND, FACING), above)
        for j, q in enumerate(RADIAL):
            cells[q, a, pl.ds(inner_pad, 1), :] = edges[round_, j, pl.ds(a, 1), :]

        def layer(qs, slot, by=0):
            return [cells[q, slot, pl.ds(PAD + by, height), :] for q in qs]

        total = [None] * 5
        here = layer(AXIAL, a)
        add_side(total, here, layer(AXIAL, above), 1, 1)
        add_side(total, here, layer(AXIAL, below), 1, -1)
        here = layer(RADIAL, a)
        add_side(total, here, layer(RADIAL, a, 1), 2, 1)
        add_side(total, here, layer(RADIAL, a, -1), 2, -1)
        for c in range(5):
            sums[c, i] = total[c]

    def rate_of(cells, round_, i):
        a = jnp.where(i == layers, OTHER, i)
        total = [sums[c, i] for c in range(5)]
        here = [cells[q, a, body, :] for q in CIRCUM]
        before = pltpu.roll(ghosts[round_, 0], lax.rem(width - a, width), 1)
        after = pltpu.roll(ghosts[round_, 1], width - 1 - a, 1)
        up, down = [], []
        for j in range(8):
            ghost = pltpu.roll(after, width - SLOTS * j, 1) if j else after
            up.append(jnp.where(lanes == width - 1, ghost, pltpu.roll(here[j], width - 1, 1)))
            ghost = pltpu.roll(before, width - SLOTS * j, 1) if j else before
            down.append(jnp.where(lanes == 0, ghost, pltpu.roll(here[j], 1, 1)))
        add_side(total, here, up, 3, 1)
        add_side(total, here, down, 3, -1)
        half = 0.5 * volumes[i]
        return a, [half * part for part in total]

    def local_copies(round_):
        return [
            pltpu.make_async_remote_copy(
                src_ref=src,
                dst_ref=dst,
                send_sem=send_sem.at[round_, i],
                recv_sem=recv_sem.at[round_, i],
                device_id=device,
                device_id_type=MESH,
            )
            for i, (src, dst, device) in enumerate(
                (
                    (packed.at[round_, 0], ghosts.at[round_, 1], left),
                    (packed.at[round_, 1], ghosts.at[round_, 0], right),
                    (rows.at[round_, :, pl.ds(0, 8)], edges.at[round_, :, pl.ds(0, 8)], beside),
                    (halves_out.at[0], halves_in.at[0], left),
                    (halves_out.at[1], halves_in.at[1], right),
                    (rows.at[round_, :, pl.ds(8, 8)], edges.at[round_, :, pl.ds(8, 8)], beside),
                )
            )
            if round_ == 0 or i < 3
        ]

    local = [local_copies(r) for r in range(2)]
    for r in range(2):
        packed[r] = jnp.zeros_like(packed[r])
        rows[r] = jnp.zeros_like(rows[r])

    def prepare(a, carry):
        pack(0, a, keep(cells0, a, [state_ref[0, c, a] for c in range(5)]))
        keep_rows(cells0, 0, a)
        volumes[a] = volume_ref[0, a]
        return carry

    lax.fori_loop(0, layers, prepare, 0)
    for c in range(11):
        split(c)
    middle = [pltpu.roll(far_ref[pick, c], half_width, 1) for c in range(5)]
    pack(0, SPARE, quantities(middle))

    pl.semaphore_wait(barrier, 3)
    for copy in local[0][:5]:
        copy.start()
    mine = [state_ref[0, c, face_layer] for c in range(5)]
    keep(cells0, FACING, other_frame(mine, sigma * wheel))
    local[0][2].wait_recv()

    def early_layers(j, carry):
        without_circ(cells0, 0, j + row)
        return carry

    lax.fori_loop(0, layers - 1, early_layers, 0)
    for i in (0, 1, 3, 4):
        local[0][i].wait_recv()

    pairs = [turned(c) for c in range(5)]
    other = [jnp.where(low_lanes, low, high) for low, high in pairs]
    keep(cells0, OTHER, other)
    keep_rows(cells0, 0, OTHER)
    local[0][5].start()
    keep(cells0, GHOST, other_frame(other, -sigma * wheel))
    keep(cells0, BEYOND, [window(5 + c) for c in range(5)])
    volumes[layers] = window(10)
    late, early = columns(
        OTHER, quantities([high for _, high in pairs]), quantities([low for low, _ in pairs])
    )
    begin = jnp.where(row == 0, rest, width - rest)
    here = lax.rem(lanes, SLOTS) == OTHER
    for side, tile, edge in ((0, early, 0), (1, late, width)):
        got = ghosts[0, side]
        spare = pltpu.roll(got, width + OTHER - SPARE, 1)
        ghosts[0, side] = jnp.where(here, jnp.where(begin == edge, spare, tile), got)

    without_circ(cells0, 0, face_layer)

    def first_section(i, carry):
        @pl.when(i == layers)
        def _():
            for copy in local[1]:
                copy.start()
            local[0][5].wait_recv()
            without_circ(cells0, 0, layers)

        a, rate = rate_of(cells0, 0, i)
        u = [cells0[c, a, body, :] + TIME_STEP * rate[c] for c in range(5)]
        turned = jnp.where(i == layers, -sigma, 0.0) * wheel
        values = keep(cells1, i, other_frame(u, turned))

        @pl.when(i < layers)
        def _():
            pack(1, i, values)
            keep_rows(cells1, 1, i)

        return carry

    lax.fori_loop(0, layers + 1, first_section, 0)
    local[1][2].wait_recv()

    def second_early(i, carry):
        without_circ(cells1, 1, i)
        return carry

    lax.fori_loop(0, layers, second_early, 0)
    local[1][0].wait_recv()
    local[1][1].wait_recv()

    def second_section(i, carry):
        _, rate = rate_of(cells1, 1, i)
        for c in range(5):
            rate_ref[0, c, i] = rate[c]
            new_ref[0, c, i] = 0.5 * cells0[c, i, body, :] + 0.5 * (
                cells1[c, i, body, :] + TIME_STEP * rate[c]
            )
        return carry

    lax.fori_loop(0, layers, second_section, 0)
    for copy in local[0] + local[1]:
        copy.wait_send()


def far(shift, state, inv_volume):
    height, width = state.shape[3:]
    anywhere = pl.BlockSpec(memory_space=pl.ANY)
    return pl.pallas_call(
        functools.partial(far_kernel, shift, lax.axis_size("circ")),
        out_shape=jax.ShapeDtypeStruct((2, 11, height, width), jnp.float32),
        in_specs=[anywhere, anywhere],
        out_specs=anywhere,
        scratch_shapes=[pltpu.SemaphoreType.DMA((3, 2)), pltpu.SemaphoreType.DMA((3, 2))],
        compiler_params=pltpu.CompilerParams(collective_id=1 + shift // 2 // GROUP * GROUP + shift % GROUP, has_side_effects=True),
    )(state, inv_volume)


def on_device(state, inv_volume, wheel_speed, offset):
    sectors = lax.axis_size("circ")
    layers, height, width = state.shape[2:]
    whole = lax.rem((offset[0] + width // 2) // width, sectors)
    arrived = lax.switch(
        whole // (2 * GROUP) * GROUP + lax.rem(whole, GROUP),
        [
            functools.partial(far, first + shift)
            for first in range(0, sectors, 2 * GROUP)
            for shift in range(GROUP)
        ],
        state,
        inv_volume,
    )
    f32 = jnp.float32
    cells = pltpu.VMEM((QUANTITIES, layers + 4, height + 2 * PAD, width), f32)
    vmem = pl.BlockSpec(memory_space=pltpu.VMEM)
    out = jax.ShapeDtypeStruct(state.shape, f32)
    return pl.pallas_call(
        functools.partial(kernel, sectors),
        out_shape=(out, out),
        in_specs=[pl.BlockSpec(memory_space=pltpu.SMEM)] + [vmem] * 4,
        out_specs=(vmem, vmem),
        scratch_shapes=[
            cells,
            cells,
            pltpu.VMEM((layers + 1, height, width), f32),
            pltpu.VMEM((5, layers + 1, height, width), f32),
            pltpu.VMEM((2, 2, height, width), f32),
            pltpu.VMEM((2, 2, height, width), f32),
            pltpu.VMEM((2, 8, SLOTS, width), f32),
            pltpu.VMEM((2, 8, SLOTS, width), f32),
            pltpu.VMEM((2, 11, height // 2, width), f32),
            pltpu.VMEM((2, 11, height // 2, width), f32),
            pltpu.SemaphoreType.DMA((2, 6)),
            pltpu.SemaphoreType.DMA((2, 6)),
        ],
        compiler_params=pltpu.CompilerParams(
            collective_id=0, has_side_effects=True, vmem_limit_bytes=32 * 2**20
        ),
    )(offset, wheel_speed[None, :], state, inv_volume, arrived)


def solution(mesh):
    return jax.shard_map(
        on_device,
        mesh=mesh,
        in_specs=(
            P("row", None, None, "rad", "circ"),
            P("row", None, "rad", "circ"),
            P("rad"),
            P(),
        ),
        out_specs=(P("row", None, None, "rad", "circ"), P("row", None, None, "rad", "circ")),
        check_vma=False,
    )
```
